256 devices in a mesh: grp: 2 (over z_hi), row: 4 (over y), tp: 32 (over z_lo, x, core).
Axes of the slice: x: 4, y: 4, z: 8 (z_hi: 2, z_lo: 4; z = z_hi * 4 + z_lo), core: 2. Of those that a mesh axis runs over, the one named last changes fastest.
Arguments:
- query: bfloat16 [32, 16384], P(('grp', 'row')), may hold values from -120 to 120
- cached_key_rows: bfloat16 [32, 8192, 1024], P(('grp', 'row'), 'tp'), may hold values from -6 to 6
- cached_value_rows: bfloat16 [32, 8192, 1024], P(('grp', 'row'), 'tp'), may hold values from -6 to 6
- row_cache_length: int32 [32], P(('grp', 'row')), may hold values from 2 to 8192, as said below
- attention_output_weight: bfloat16 [16384, 16384], P('tp', 'row'), may hold values from -1.5 to 1.5
- resid: bfloat16 [32, 16384], P('grp', ('row', 'tp')), may hold values from -16 to 16
- feed_norm_scale: bfloat16 [16384], P(('row', 'tp')), may hold values from 0.5 to 1.5
- gate_down_weight: bfloat16 [16384, 1024], P(('row', 'tp')), may hold values from -0.046875 to 0.046875
- up_down_weight: bfloat16 [16384, 1024], P(('row', 'tp')), may hold values from -0.046875 to 0.046875
- gate_expansion_weight: bfloat16 [1024, 53248], P('grp', 'tp'), may hold values from -1.5 to 1.5
- up_expansion_weight: bfloat16 [1024, 53248], P('grp', 'tp'), may hold values from -1.5 to 1.5
- row_adapter_index: int32 [32], replicated, may hold values from 0 to 63
Outputs:
- stream: bfloat16 [32, 16384], P('grp', ('row', 'tp'))
- gate_delta: bfloat16 [32, 53248], P(('grp', 'row'), 'tp')
- up_delta: bfloat16 [32, 53248], P(('grp', 'row'), 'tp')
The draws below stay inside these ranges and needn't reach their ends.
Inputs may be any that keep to these rules, and one draw needn't show every extreme that they name: `row_cache_length`: some row has all 8192 positions live.
All inputs are finite; a program needn't handle non-finite values.
Results may differ from the reference program's by a relative error of at most 0.011.
Values may be sent and summed in bfloat16 or wider, within the bound.
A program may use at most 128 MiB of HBM per device.

```python
import math
import jax
import jax.numpy as jnp
from jax import lax

MODEL_WIDTH = 16384
HIDDEN_UNITS = 53248
HQ = 128
KVH = 8
HD = 128
ADAPTER_RANK = 16
ADAPTER_COUNT = 64
CTX_DEV = 256
CTX = 8192
ROWS = 32
N_TP = 32


def shared_first(key):
    return jnp.clip(jax.random.normal(jax.random.fold_in(key, 11), (ROWS, KVH * HD), jnp.float32), -6.0, 6.0)


def draw_cached_key_rows(key, part):
    first_keys = shared_first(key)
    key = jax.random.fold_in(key, 3)
    keys_all = jnp.clip(jax.random.normal(key, (ROWS, CTX, KVH * HD), jnp.float32), -6.0, 6.0)
    keys_all = keys_all.at[:, 0].set(first_keys)
    return keys_all.astype(jnp.bfloat16)


def draw_query(key, part):
    key = jax.random.fold_in(key, 5)
    values = jnp.clip(jax.random.normal(key, (ROWS, HQ * HD), jnp.float32), -6.0, 6.0)
    return values.astype(jnp.bfloat16)


def draw_row_cache_length(key, part):
    key = jax.random.fold_in(key, 7)
    first, second = jax.random.split(key)
    lengths = jax.random.randint(first, (ROWS,), 2, CTX + 1, jnp.int32)
    full_row = jax.random.randint(second, (), 0, ROWS, jnp.int32)
    return lengths.at[full_row].set(CTX)


def draw_resid(key, part):
    key = jax.random.fold_in(key, 21)
    first, second, third = jax.random.split(key, 3)
    ramp = 3.0 ** (0.5 * jnp.arange(MODEL_WIDTH, dtype=jnp.float32) / (MODEL_WIDTH - 1))
    column = jnp.exp(jax.random.uniform(second, (1, MODEL_WIDTH), jnp.float32, 0.0, math.log(3.2))) * ramp[None, :] / 2.5
    scale_rows = jnp.exp(jax.random.uniform(third, (ROWS, 1), jnp.float32, math.log(0.5), math.log(1.6)))
    base = jax.random.normal(first, (ROWS, MODEL_WIDTH), jnp.float32)
    return jnp.clip(base * column * scale_rows, -16.0, 16.0).astype(jnp.bfloat16)


def place_ends(entries, key, smallest, largest):
    spot = [jax.random.randint(jax.random.fold_in(key, axis), (), 0, length) for axis, length in enumerate(entries.shape)]
    widest = entries.shape.index(max(entries.shape))
    neighbour = spot[:widest] + [(spot[widest] + 1) % entries.shape[widest]] + spot[widest + 1:]
    return entries.at[tuple(spot)].set(smallest).at[tuple(neighbour)].set(largest)


def block_scale(own_key, shape, pieces, smallest, high):
    def one(dim, shards_of):
        steps = jax.random.uniform(jax.random.fold_in(jax.random.fold_in(own_key, 6), dim), (shards_of,), jnp.float32, smallest / len(pieces), high / len(pieces))
        return jnp.repeat(jnp.exp(steps), shape[dim] // shards_of).reshape((-1,) + (1,) * (len(shape) - dim - 1))

    loudness = one(*pieces[0])
    for cut in pieces[1:]:
        loudness = loudness * one(*cut)
    return loudness


def gaussian(rng, shape, deviation, reach, shards=(), held_as=jnp.bfloat16):
    loudness = block_scale(rng, shape, shards, -0.22, 0.18) if shards else 1.0
    array = jax.random.normal(rng, shape, jnp.float32) * deviation * loudness
    return jnp.minimum(jnp.maximum(array, -reach), reach).astype(held_as)


def setup_inputs(seed: int = 0) -> dict:
    key_of = jax.random.split(jax.random.key(seed), 13)
    query = draw_query(jax.random.fold_in(key_of[12], 71), 0)
    cached_key_rows = draw_cached_key_rows(jax.random.fold_in(key_of[12], 71), 0)
    cached_value_rows = gaussian(key_of[2], (ROWS, CTX, KVH * HD), 1.0, 6.0, ((0, 8), (1, 32)))
    row_cache_length = draw_row_cache_length(jax.random.fold_in(key_of[12], 71), 0)
    attention_output_weight = gaussian(key_of[4], (MODEL_WIDTH, MODEL_WIDTH), 0.25, 1.5, ((0, 32), (1, 4)))
    resid = draw_resid(jax.random.fold_in(key_of[12], 71), 0)
    feed_norm_scale = jnp.clip(1.0 + 0.1 * jax.random.normal(key_of[6], (MODEL_WIDTH,), jnp.float32), 0.5, 1.5).astype(jnp.bfloat16)
    gate_down_weight = gaussian(key_of[7], (MODEL_WIDTH, ADAPTER_COUNT * ADAPTER_RANK), MODEL_WIDTH ** -0.5, 0.046875, ((0, 128),))
    up_down_weight = gaussian(key_of[8], (MODEL_WIDTH, ADAPTER_COUNT * ADAPTER_RANK), MODEL_WIDTH ** -0.5, 0.046875, ((0, 128),))
    gate_expansion_weight = gaussian(key_of[9], (ADAPTER_COUNT * ADAPTER_RANK, HIDDEN_UNITS), ADAPTER_RANK ** -0.5, 1.5, ((0, 2), (1, 32)))
    up_expansion_weight = gaussian(key_of[10], (ADAPTER_COUNT * ADAPTER_RANK, HIDDEN_UNITS), ADAPTER_RANK ** -0.5, 1.5, ((0, 2), (1, 32)))
    row_adapter_index = place_ends(jax.random.randint(key_of[11], (ROWS,), 0, ADAPTER_COUNT), jax.random.fold_in(key_of[11], 1), 0, ADAPTER_COUNT - 1).astype(jnp.int32)
    return dict(query=query, cached_key_rows=cached_key_rows, cached_value_rows=cached_value_rows, row_cache_length=row_cache_length, attention_output_weight=attention_output_weight, resid=resid, feed_norm_scale=feed_norm_scale, gate_down_weight=gate_down_weight, up_down_weight=up_down_weight, gate_expansion_weight=gate_expansion_weight, up_expansion_weight=up_expansion_weight, row_adapter_index=row_adapter_index)


epsilon = 1e-05

def attend_row(inputs):
    query_row, key_row, value_row, length = inputs
    group = HQ // KVH
    query_heads = query_row.astype(jnp.float32).reshape(KVH, group, HD)
    key_blocks = key_row.astype(jnp.float32).reshape(N_TP, CTX_DEV, KVH, HD)
    value_blocks = value_row.astype(jnp.float32).reshape(N_TP, CTX_DEV, KVH, HD)
    scores = jnp.einsum('kgd,bpkd->kgbp', query_heads, key_blocks) * HD ** (-0.5)
    position = jnp.arange(CTX, dtype=jnp.int32).reshape(N_TP, CTX_DEV)
    visible = position < length
    masked = jnp.where(visible, scores, -1e+30)
    highest = lax.optimization_barrier(jnp.max(masked, axis=-1))
    weights = jnp.where(visible, jnp.exp(masked - highest[..., None]), 0.0)
    totals = lax.optimization_barrier(jnp.sum(weights, axis=-1))
    probabilities = weights.astype(jnp.bfloat16)
    accumulated = jnp.einsum('kgbp,bpkd->kgbd', probabilities.astype(jnp.float32), value_blocks)
    overall = lax.optimization_barrier(jnp.max(highest, axis=-1))
    factor = jnp.exp(highest - overall[..., None])
    normal_sum = lax.optimization_barrier(jnp.sum(totals * factor, axis=-1))
    combined = lax.optimization_barrier(jnp.sum(accumulated * factor[..., None], axis=2))
    return (combined / normal_sum[..., None]).reshape(MODEL_WIDTH).astype(jnp.bfloat16)

def reference(query, cached_key_rows, cached_value_rows, row_cache_length, attention_output_weight, resid, feed_norm_scale, gate_down_weight, up_down_weight, gate_expansion_weight, up_expansion_weight, row_adapter_index):
    attended = lax.map(attend_row, (query, cached_key_rows, cached_value_rows, row_cache_length))
    projected = jnp.dot(attended, attention_output_weight, preferred_element_type=jnp.float32)
    hidden = resid.astype(jnp.float32) + projected
    stream = hidden.astype(jnp.bfloat16)
    inverse_norm = lax.rsqrt(lax.optimization_barrier(jnp.sum(hidden * hidden, axis=1)) / MODEL_WIDTH + epsilon)
    scaled_input = (hidden * feed_norm_scale.astype(jnp.float32)[None, :]).astype(jnp.bfloat16)
    chosen = (row_adapter_index[:, None] == jnp.arange(ADAPTER_COUNT, dtype=jnp.int32)[None, :]).astype(jnp.float32)

    def selected_adapter_slots(table):
        product = jnp.dot(scaled_input, table, preferred_element_type=jnp.float32)
        return lax.optimization_barrier(jnp.sum(product.reshape(ROWS, ADAPTER_COUNT, ADAPTER_RANK) * chosen[:, :, None], axis=1))
    gate_rank_rows = (selected_adapter_slots(gate_down_weight) * inverse_norm[:, None]).astype(jnp.bfloat16)
    up_rank_rows = (selected_adapter_slots(up_down_weight) * inverse_norm[:, None]).astype(jnp.bfloat16)

    def expand_rows(rank_part, table):
        coefficient = (chosen[:, :, None] * rank_part.astype(jnp.float32)[:, None, :]).reshape(ROWS, ADAPTER_COUNT * ADAPTER_RANK).astype(jnp.bfloat16)
        return jnp.dot(coefficient, table, preferred_element_type=jnp.float32).astype(jnp.bfloat16)
    return (stream, expand_rows(gate_rank_rows, gate_expansion_weight), expand_rows(up_rank_rows, up_expansion_weight))
```

```python
import functools

import jax
import jax.numpy as jnp
from jax import lax
from jax.experimental import pallas as pl
from jax.experimental.pallas import tpu as pltpu
from jax.sharding import PartitionSpec as P

HD = 128
RANK = 16
EPSILON = 1e-05
MESH = pl.DeviceIdType.MESH
F32 = jnp.float32
BF16 = jnp.bfloat16


def iota(shape, axis):
    return lax.broadcasted_iota(jnp.int32, shape, axis)


def kernel(
    sizes,
    lengths,
    ids,
    query_hbm,
    key_hbm,
    value_hbm,
    wo_hbm,
    resid_hbm,
    gain_hbm,
    gate_down_hbm,
    up_down_hbm,
    gate_exp_hbm,
    up_exp_hbm,
    stream_out,
    gate_out,
    up_out,
    query,
    keys,
    values,
    wo,
    resid,
    gain,
    down,
    expand,
    acc_s,
    stat_s,
    msg_s,
    send_b,
    send_st,
    recv_b,
    recv_st,
    recv_c,
    send_d,
    recv_d,
    send_e,
    recv_e,
    recv_g,
    send_f,
    recv_f,
    load_sem,
    kv_sem,
    send_sem,
    recv_sem,
):
    n_grp, n_row, n_tp = sizes
    rows, positions, kv_width = keys.shape
    kv_heads = kv_width // HD
    heads = query.shape[1] // HD
    group = heads // kv_heads
    per = heads // n_tp
    tile = rows * per
    micro_rows = n_row * rows
    grp = lax.axis_index("grp")
    row = lax.axis_index("row")
    me = lax.axis_index("tp")

    def load(source, target, index):
        copy = pltpu.make_async_copy(source, target, load_sem.at[index])
        copy.start()
        return copy

    def wait_bytes(ref, sem):
        pltpu.make_async_copy(ref, ref, sem).wait()

    query_copy = load(query_hbm, query, 0)
    kv_copies = []
    for b in range(rows):
        pair = (
            pltpu.make_async_copy(key_hbm.at[b], keys.at[b], kv_sem.at[0, b]),
            pltpu.make_async_copy(value_hbm.at[b], values.at[b], kv_sem.at[1, b]),
        )
        for copy in pair:
            copy.start()
        kv_copies.append(pair)
    wo_copy = load(wo_hbm, wo, 1)
    resid_copy = load(resid_hbm, resid, 2)
    gain_copy = load(gain_hbm, gain, 3)
    down_copies = (load(gate_down_hbm, down.at[0], 4), load(up_down_hbm, down.at[1], 5))
    expand_copies = (load(gate_exp_hbm, expand.at[0], 6), load(up_exp_hbm, expand.at[1], 7))

    barrier = pltpu.get_barrier_semaphore()
    for k in range(1, n_row):
        pl.semaphore_signal(
            barrier, inc=1, device_id={"row": lax.rem(row + k, n_row)}, device_id_type=MESH
        )

    def greet(k, carry):
        there = lax.rem(me + k, n_tp)

        @pl.when(k > 0)
        def _():
            pl.semaphore_signal(barrier, inc=1, device_id={"tp": there}, device_id_type=MESH)

        pl.semaphore_signal(
            barrier, inc=1, device_id={"grp": 1 - grp, "tp": there}, device_id_type=MESH
        )
        return carry

    lax.fori_loop(0, n_tp, greet, 0)

    query_copy.wait()
    head_rows = query[...].astype(F32).reshape(rows, heads, HD).astype(BF16)
    position = me * positions + iota((heads, positions), 1)
    stat_lane = iota((heads, HD), 1) - rows * lax.rem(iota((heads, HD), 0), per)
    stats = jnp.zeros((heads, HD), F32)
    for b in range(rows):
        for copy in kv_copies[b]:
            copy.wait()
        scores = jnp.concatenate(
            [
                lax.dot_general(
                    head_rows[b, k * group : (k + 1) * group],
                    keys[b, :, k * HD : (k + 1) * HD],
                    (((1,), (1,)), ((), ())),
                    preferred_element_type=F32,
                )
                for k in range(kv_heads)
            ],
            axis=0,
        ) * (HD ** (-0.5))
        visible = position < lengths[b]
        masked = jnp.where(visible, scores, -1e30)
        highest = jnp.max(masked, axis=1, keepdims=True)
        weights = jnp.where(visible, jnp.exp(masked - highest), 0.0)
        total = jnp.sum(weights, axis=1, keepdims=True)
        weights = weights.astype(BF16)
        for k in range(kv_heads):
            acc_s[b, k * group : (k + 1) * group, :] = jnp.dot(
                weights[k * group : (k + 1) * group],
                values[b, :, k * HD : (k + 1) * HD],
                preferred_element_type=F32,
            )
        stats = jnp.where(stat_lane == b, highest, stats)
        stats = jnp.where(stat_lane == tile + b, total, stats)
        for j in range(per):
            msg_s[pl.ds(j * rows + b, n_tp, stride=tile), :] = acc_s[
                b, pl.ds(j, n_tp, stride=per), :
            ]
    send_b[...] = msg_s[...].reshape(n_tp, tile, HD).astype(BF16)
    stat_s[...] = stats
    stat_rows = stat_s[pl.ds(0, n_tp, stride=per), :]
    for j in range(1, per):
        stat_rows += stat_s[pl.ds(j, n_tp, stride=per), :]
    send_st[...] = stat_rows.reshape(n_tp, 1, HD)

    pl.semaphore_wait(barrier, n_row - 1 + 2 * n_tp - 1)

    def remote(source, target, index, device):
        return pltpu.make_async_remote_copy(
            src_ref=source,
            dst_ref=target,
            send_sem=send_sem.at[index],
            recv_sem=recv_sem.at[index],
            device_id=device,
            device_id_type=MESH,
        )

    def send_partial(k, carry):
        there = lax.rem(me + k, n_tp)
        remote(send_st.at[there], recv_st.at[k - 1], 1, {"tp": there}).start()
        remote(send_b.at[there], recv_b.at[k - 1], 0, {"tp": there}).start()
        return carry

    lax.fori_loop(1, n_tp, send_partial, 0)
    recv_b[n_tp - 1] = send_b[me]
    recv_st[n_tp - 1] = send_st[me]
    wait_bytes(recv_st.at[0 : n_tp - 1], recv_sem.at[1])

    part_stats = recv_st[...].reshape(n_tp, HD)
    overall = jnp.max(part_stats, axis=0, keepdims=True)
    factor = jnp.exp(part_stats - overall)
    part_totals = pltpu.roll(part_stats, HD - tile, 1)
    normal = jnp.sum(factor * part_totals, axis=0, keepdims=True)
    share = jnp.where(iota((n_tp, HD), 1) < tile, factor / normal, 0.0)
    share = share.T[:tile]
    wait_bytes(recv_b.at[0 : n_tp - 1], recv_sem.at[0])
    attended = jnp.zeros((tile, HD), F32)
    for s in range(n_tp):
        attended += share[:, s : s + 1] * recv_b[s].astype(F32)

    recv_c[row] = attended.astype(BF16)
    for k in range(1, n_row):
        remote(recv_c.at[row], recv_c.at[row], 2, {"row": lax.rem(row + k, n_row)}).start()
    wait_bytes(recv_c.at[0 : n_row - 1], recv_sem.at[2])
    gathered = recv_c[...].astype(F32)
    left = jnp.concatenate(
        [
            jnp.concatenate(
                [gathered[r, j * rows : (j + 1) * rows] for r in range(n_row)], axis=0
            )
            for j in range(per)
        ],
        axis=1,
    ).astype(BF16)

    wo_copy.wait()

    def project(k, carry):
        pair = lax.rem(lax.div(me, 2) + k, n_tp // 2)
        columns = pl.ds(pl.multiple_of(pair * 2 * HD, 2 * HD), 2 * HD)
        product = jnp.dot(left, wo[:, columns], preferred_element_type=F32).astype(BF16)
        for half in range(2):
            there = pair * 2 + half
            send_d[there] = product[:, half * HD : (half + 1) * HD]
            distance = lax.rem(there - me + n_tp, n_tp)

            @pl.when(distance > 0)
            def _():
                remote(send_d.at[there], recv_d.at[distance - 1], 3, {"tp": there}).start()

        return carry

    lax.fori_loop(1, n_tp // 2 + 1, project, 0)
    recv_d[n_tp - 1] = send_d[me]

    def id_column(base, count, shape, start, column):
        for i in range(count):
            column = jnp.where(iota(shape, 0) == start + i, ids[base + i], column)
        return column

    micro_ids = id_column(
        grp * micro_rows, micro_rows, (micro_rows, HD), 0, jnp.zeros((micro_rows, HD), jnp.int32)
    )
    lane_adapter = lax.div(iota((micro_rows, HD), 1), RANK)
    resid_copy.wait()
    gain_copy.wait()
    for copy in down_copies:
        copy.wait()
    wait_bytes(recv_d.at[0 : n_tp - 1], recv_sem.at[3])
    hidden = resid[...].astype(F32)
    projected = recv_d[0].astype(F32)
    for s in range(1, n_tp):
        projected += recv_d[s].astype(F32)
    hidden = hidden + projected
    stream_out[...] = hidden.astype(BF16)
    squares = jnp.sum(hidden * hidden, axis=1, keepdims=True)
    scaled = (hidden * gain[...].astype(F32).reshape(1, HD)).astype(BF16)

    def selected(table):
        product = jnp.dot(scaled, table, preferred_element_type=F32)
        per_chunk = HD // RANK
        chosen = jnp.zeros((micro_rows, HD), F32)
        for c in range(product.shape[1] // HD):
            chosen += jnp.where(
                lane_adapter + c * per_chunk == micro_ids, product[:, c * HD : (c + 1) * HD], 0.0
            )
        shift = HD // 2
        while shift >= RANK:
            chosen += pltpu.roll(chosen, shift, 1)
            shift //= 2
        return chosen

    lane = iota((micro_rows, HD), 1)
    part = jnp.where(
        lane < RANK,
        selected(down[0]),
        jnp.where(
            lane < 2 * RANK, selected(down[1]), jnp.where(lane == 2 * RANK, squares, 0.0)
        ),
    )

    for r in range(n_row):
        send_e[r] = part[r * rows : (r + 1) * rows]
    for k in range(1, n_row):
        there = lax.rem(row + k, n_row)
        remote(send_e.at[there], recv_e.at[k - 1], 4, {"row": there}).start()
    recv_e[n_row - 1] = send_e[row]
    wait_bytes(recv_e.at[0 : n_row - 1], recv_sem.at[4])
    summed = recv_e[0]
    for s in range(1, n_row):
        summed += recv_e[s]

    recv_g[n_tp - 1] = summed

    def spread(k, carry):
        there = lax.rem(me + k, n_tp)

        @pl.when(k > 0)
        def _():
            remote(recv_g.at[n_tp - 1], recv_g.at[k - 1], 5, {"tp": there}).start()

        remote(
            recv_g.at[n_tp - 1], recv_g.at[n_tp + k], 6, {"grp": 1 - grp, "tp": there}
        ).start()
        return carry

    lax.fori_loop(0, n_tp, spread, 0)
    both = 2 * rows
    pair_ids = id_column(
        grp * micro_rows + row * rows, rows, (both, HD), 0, jnp.zeros((both, HD), jnp.int32)
    )
    pair_ids = id_column(
        (1 - grp) * micro_rows + row * rows, rows, (both, HD), rows, pair_ids
    )
    half_adapters = expand.shape[1] // RANK
    local_ids = pair_ids - grp * half_adapters
    pair_adapter = lax.div(iota((both, HD), 1), RANK)
    for copy in expand_copies:
        copy.wait()
    wait_bytes(recv_g.at[0 : n_tp - 1], recv_sem.at[5])
    wait_bytes(recv_g.at[n_tp : 2 * n_tp], recv_sem.at[6])
    sums = []
    for half in range(2):
        sum_half = recv_g[half * n_tp]
        for s in range(1, n_tp):
            sum_half += recv_g[half * n_tp + s]
        sums.append(sum_half)
    sums = jnp.concatenate(sums, axis=0)
    inverse = lax.rsqrt(sums[:, 2 * RANK : 2 * RANK + 1] / (n_row * n_tp * HD) + EPSILON)
    ranks = (sums * inverse).astype(BF16).astype(F32)
    pair_lane = iota((both, HD), 1)

    deltas = []
    for which in range(2):
        spread_rank = ranks if which == 0 else pltpu.roll(ranks, HD - RANK, 1)
        spread_rank = jnp.where(pair_lane < RANK, spread_rank, 0.0)
        shift = RANK
        while shift < HD:
            spread_rank += pltpu.roll(spread_rank, shift, 1)
            shift *= 2
        per_chunk = HD // RANK
        coefficient = jnp.concatenate(
            [
                jnp.where(pair_adapter + c * per_chunk == local_ids, spread_rank, 0.0)
                for c in range(half_adapters // per_chunk)
            ],
            axis=1,
        ).astype(BF16)
        deltas.append(jnp.dot(coefficient, expand[which], preferred_element_type=F32))

    chunks = deltas[0].shape[1] // HD
    stack = recv_f.shape[1] // rows
    pieces = [
        deltas[which][rows:, c * HD : (c + 1) * HD] for which in range(2) for c in range(chunks)
    ]
    pieces += [jnp.zeros((rows, HD), F32)] * (-len(pieces) % stack)
    for i in range(len(pieces) // stack):
        send_f[i] = jnp.concatenate(pieces[i * stack : (i + 1) * stack], axis=0).astype(BF16)
    remote(send_f, recv_f, 7, {"grp": 1 - grp}).start()
    wait_bytes(recv_f, recv_sem.at[7])
    outs = (gate_out, up_out)
    for which in range(2):
        for c in range(chunks):
            at = which * chunks + c
            other = recv_f[at // stack].astype(F32)[at % stack * rows : (at % stack + 1) * rows]
            own = deltas[which][:rows, c * HD : (c + 1) * HD].astype(BF16).astype(F32)
            outs[which][:, c * HD : (c + 1) * HD] = (own + other).astype(BF16)

    wait_bytes(recv_b.at[0 : n_tp - 1], send_sem.at[0])
    wait_bytes(recv_st.at[0 : n_tp - 1], send_sem.at[1])
    wait_bytes(recv_c.at[0 : n_row - 1], send_sem.at[2])
    wait_bytes(recv_d.at[0 : n_tp - 1], send_sem.at[3])
    wait_bytes(recv_e.at[0 : n_row - 1], send_sem.at[4])
    wait_bytes(recv_g.at[0 : n_tp - 1], send_sem.at[5])
    wait_bytes(recv_g.at[n_tp : 2 * n_tp], send_sem.at[6])
    wait_bytes(send_f, send_sem.at[7])


def layer(
    sizes,
    query,
    cached_key_rows,
    cached_value_rows,
    row_cache_length,
    attention_output_weight,
    resid,
    feed_norm_scale,
    gate_down_weight,
    up_down_weight,
    gate_expansion_weight,
    up_expansion_weight,
    row_adapter_index,
):
    n_grp, n_row, n_tp = sizes
    rows = query.shape[0]
    heads = query.shape[1] // HD
    tile = rows * (heads // n_tp)
    columns = gate_expansion_weight.shape[1]
    stack = 16 // rows
    packed = -(-2 * (columns // HD) // stack)
    smem = pl.BlockSpec(memory_space=pltpu.SMEM)
    hbm = pl.BlockSpec(memory_space=pl.ANY)
    vmem = pl.BlockSpec(memory_space=pltpu.VMEM)
    return pl.pallas_call(
        functools.partial(kernel, sizes),
        out_shape=(
            jax.ShapeDtypeStruct(resid.shape, BF16),
            jax.ShapeDtypeStruct((rows, columns), BF16),
            jax.ShapeDtypeStruct((rows, columns), BF16),
        ),
        in_specs=[smem] * 2 + [hbm] * 10,
        out_specs=(vmem,) * 3,
        scratch_shapes=[
            pltpu.VMEM(query.shape, BF16),
            pltpu.VMEM(cached_key_rows.shape, BF16),
            pltpu.VMEM(cached_value_rows.shape, BF16),
            pltpu.VMEM(attention_output_weight.shape, BF16),
            pltpu.VMEM(resid.shape, BF16),
            pltpu.VMEM(feed_norm_scale.shape, BF16),
            pltpu.VMEM((2,) + gate_down_weight.shape, BF16),
            pltpu.VMEM((2,) + gate_expansion_weight.shape, BF16),
            pltpu.VMEM((rows, heads, HD), F32),
            pltpu.VMEM((heads, HD), F32),
            pltpu.VMEM((n_tp * tile, HD), F32),
            pltpu.VMEM((n_tp, tile, HD), BF16),
            pltpu.VMEM((n_tp, 1, HD), F32),
            pltpu.VMEM((n_tp, tile, HD), BF16),
            pltpu.VMEM((n_tp, 1, HD), F32),
            pltpu.VMEM((n_row, tile, HD), BF16),
            pltpu.VMEM((n_tp, n_row * rows, HD), BF16),
            pltpu.VMEM((n_tp, n_row * rows, HD), BF16),
            pltpu.VMEM((n_row, rows, HD), F32),
            pltpu.VMEM((n_row, rows, HD), F32),
            pltpu.VMEM((2 * n_tp, rows, HD), F32),
            pltpu.VMEM((packed, 16, HD), BF16),
            pltpu.VMEM((packed, 16, HD), BF16),
            pltpu.SemaphoreType.DMA((8,)),
            pltpu.SemaphoreType.DMA((2, rows)),
            pltpu.SemaphoreType.DMA((8,)),
            pltpu.SemaphoreType.DMA((8,)),
        ],
        compiler_params=pltpu.CompilerParams(
            collective_id=0, has_side_effects=True, vmem_limit_bytes=56 * 1024 * 1024
        ),
    )(
        row_cache_length,
        row_adapter_index,
        query,
        cached_key_rows,
        cached_value_rows,
        attention_output_weight,
        resid,
        feed_norm_scale,
        gate_down_weight,
        up_down_weight,
        gate_expansion_weight,
        up_expansion_weight,
    )


def solution(mesh):
    sizes = tuple(mesh.shape[axis] for axis in ("grp", "row", "tp"))
    return jax.shard_map(
        functools.partial(layer, sizes),
        mesh=mesh,
        in_specs=(
            P(("grp", "row"), None),
            P(("grp", "row"), "tp", None),
            P(("grp", "row"), "tp", None),
            P(("grp", "row")),
            P("tp", "row"),
            P("grp", ("row", "tp")),
            P(("row", "tp")),
            P(("row", "tp"), None),
            P(("row", "tp"), None),
            P("grp", "tp"),
            P("grp", "tp"),
            P(),
        ),
        out_specs=(P("grp", ("row", "tp")), P(("grp", "row"), "tp"), P(("grp", "row"), "tp")),
        check_vma=False,
    )
```

```python
import functools

import jax
import jax.numpy as jnp
from jax import lax
from jax.experimental import pallas as pl
from jax.experimental.pallas import tpu as pltpu
from jax.sharding import PartitionSpec as P

HD = 128
RANK = 16
EPSILON = 1e-05
MESH = pl.DeviceIdType.MESH
F32 = jnp.float32
BF16 = jnp.bfloat16


def iota(shape, axis):
    return lax.broadcasted_iota(jnp.int32, shape, axis)


def kernel(
    sizes,
    lengths,
    ids,
    query_hbm,
    key_hbm,
    value_hbm,
    wo_hbm,
    resid_hbm,
    gain_hbm,
    gate_down_hbm,
    up_down_hbm,
    gate_exp_hbm,
    up_exp_hbm,
    stream_out,
    gate_out,
    up_out,
    query,
    keys,
    values,
    wo,
    resid,
    gain,
    down,
    expand,
    weights_s,
    acc_s,
    share_s,
    stat_s,
    msg_s,
    send_b,
    send_st,
    recv_b,
    recv_st,
    recv_c,
    send_d,
    recv_d,
    send_e,
    recv_e,
    recv_g,
    send_f,
    recv_f,
    chosen_rows,
    load_sem,
    kv_sem,
    send_sem,
    recv_sem,
):
    n_grp, n_row, n_tp = sizes
    rows, positions, kv_width = keys.shape
    kv_heads = kv_width // HD
    heads = query.shape[1] // HD
    group = heads // kv_heads
    per = heads // n_tp
    tile = rows * per
    micro_rows = n_row * rows
    grp = lax.axis_index("grp")
    row = lax.axis_index("row")
    me = lax.axis_index("tp")

    def load(source, target, index):
        copy = pltpu.make_async_copy(source, target, load_sem.at[index])
        copy.start()
        return copy

    def wait_bytes(ref, sem):
        pltpu.make_async_copy(ref, ref, sem).wait()

    quarter = n_tp // 4
    plane = lax.div(me, quarter)
    place = lax.rem(me, quarter)
    n_core = min(2, quarter)
    n_x = quarter // n_core
    place_x = lax.div(place, n_core)
    core = lax.rem(place, n_core)
    n_near = 4 * n_core

    def other_plane(turn):
        high = lax.rem(lax.div(plane, 2) + turn // 2, 2)
        return 2 * high + lax.rem(plane + turn % 2, 2)

    def ahead(there):
        return lax.rem(there - me + n_tp, n_tp)

    query_copy = load(query_hbm, query, 0)
    key_copies = [
        pltpu.make_async_copy(key_hbm.at[b], keys.at[b], kv_sem.at[0, b]) for b in range(rows)
    ]
    value_copies = [
        pltpu.make_async_copy(value_hbm.at[b], values.at[b], kv_sem.at[1, b]) for b in range(rows)
    ]
    for copy in key_copies + value_copies:
        copy.start()

    barrier = pltpu.get_barrier_semaphore()

    def same_plane(dx):
        return plane * quarter + lax.rem(place_x + dx, n_x) * n_core + core

    def same_column(i):
        there = lax.rem(plane + i // n_core, 4) * quarter + place_x * n_core
        return there + lax.rem(core + i % n_core, n_core)

    def greet(k, carry):
        there = lax.rem(me + k, n_tp)
        pl.semaphore_signal(barrier, inc=1, device_id={"tp": there}, device_id_type=MESH)
        return carry

    for i in range(n_near):
        pl.semaphore_signal(
            barrier,
            inc=1,
            device_id={"grp": 1 - grp, "tp": same_column(i)},
            device_id_type=MESH,
        )
    lax.fori_loop(1, n_tp, greet, 0)
    for dr in range(1, n_row):
        for dx in range(n_x):
            pl.semaphore_signal(
                barrier,
                inc=1,
                device_id={"row": lax.rem(row + dr, n_row), "tp": same_plane(dx)},
                device_id_type=MESH,
            )

    query_copy.wait()
    head_rows = query[...].astype(F32).reshape(rows, heads, HD).astype(BF16)
    position = me * positions + iota((heads, positions), 1)
    stat_lane = iota((heads, HD), 1) - rows * lax.rem(iota((heads, HD), 0), per)
    stats = jnp.zeros((heads, HD), F32)
    for b in range(rows):
        key_copies[b].wait()
        scores = jnp.concatenate(
            [
                lax.dot_general(
                    head_rows[b, k * group : (k + 1) * group],
                    keys[b, :, k * HD : (k + 1) * HD],
                    (((1,), (1,)), ((), ())),
                    preferred_element_type=F32,
                )
                for k in range(kv_heads)
            ],
            axis=0,
        ) * (HD ** (-0.5))
        visible = position < lengths[b]
        masked = jnp.where(visible, scores, -1e30)
        highest = jnp.max(masked, axis=1, keepdims=True)
        weights = jnp.where(visible, jnp.exp(masked - highest), 0.0)
        total = jnp.sum(weights, axis=1, keepdims=True)
        weights_s[b] = weights.astype(BF16)
        stats = jnp.where(stat_lane == b, highest, stats)
        stats = jnp.where(stat_lane == tile + b, total, stats)
    stat_s[...] = stats
    stat_rows = stat_s[pl.ds(0, n_tp, stride=per), :]
    for j in range(1, per):
        stat_rows += stat_s[pl.ds(j, n_tp, stride=per), :]
    send_st[...] = stat_rows.reshape(n_tp, 1, HD)

    pl.semaphore_wait(barrier, n_tp - 1 + (n_row - 1) * n_x + n_near)

    def remote(source, target, index, device):
        return pltpu.make_async_remote_copy(
            src_ref=source,
            dst_ref=target,
            send_sem=send_sem.at[index],
            recv_sem=recv_sem.at[index],
            device_id=device,
            device_id_type=MESH,
        )

    def send_stats(k, carry):
        there = lax.rem(me + k, n_tp)
        remote(send_st.at[there], recv_st.at[k - 1], 1, {"tp": there}).start()
        return carry

    lax.fori_loop(1, n_tp, send_stats, 0)
    recv_st[n_tp - 1] = send_st[me]
    wo_copy = load(wo_hbm, wo, 1)
    resid_copy = load(resid_hbm, resid, 2)
    gain_copy = load(gain_hbm, gain, 3)
    down_copies = (load(gate_down_hbm, down.at[0], 4), load(up_down_hbm, down.at[1], 5))
    expand_copies = (load(gate_exp_hbm, expand.at[0], 6), load(up_exp_hbm, expand.at[1], 7))

    for b in range(rows):
        value_copies[b].wait()
        weights = weights_s[b]
        for k in range(kv_heads):
            acc_s[b, k * group : (k + 1) * group, :] = jnp.dot(
                weights[k * group : (k + 1) * group],
                values[b, :, k * HD : (k + 1) * HD],
                preferred_element_type=F32,
            )
        for j in range(per):
            msg_s[pl.ds(j * rows + b, n_tp, stride=tile), :] = acc_s[
                b, pl.ds(j, n_tp, stride=per), :
            ]
    send_b[...] = msg_s[...].reshape(n_tp, tile, HD).astype(BF16)

    def send_partial(k, carry):
        there = lax.rem(me + k, n_tp)
        remote(send_b.at[there], recv_b.at[k - 1], 0, {"tp": there}).start()
        return carry

    lax.fori_loop(1, n_tp, send_partial, 0)
    recv_b[n_tp - 1] = send_b[me]

    wait_bytes(recv_st.at[0 : n_tp - 1], recv_sem.at[1])
    part_stats = recv_st[...].reshape(n_tp, HD)
    overall = jnp.max(part_stats, axis=0, keepdims=True)
    factor = jnp.exp(part_stats - overall)
    part_totals = pltpu.roll(part_stats, HD - tile, 1)
    normal = jnp.sum(factor * part_totals, axis=0, keepdims=True)
    share = jnp.where(iota((n_tp, HD), 1) < tile, factor / normal, 0.0)
    share = share.T[:tile]
    for s in range(n_tp):
        share_s[s] = jnp.broadcast_to(share[:, s : s + 1], (tile, HD))
    wait_bytes(recv_b.at[0 : n_tp - 1], recv_sem.at[0])
    attended = share_s[0] * recv_b[0].astype(F32)
    for s in range(1, n_tp):
        attended += share_s[s] * recv_b[s].astype(F32)

    recv_c[row] = attended.astype(BF16)
    for k in range(1, n_row):
        remote(recv_c.at[row], recv_c.at[row], 2, {"row": lax.rem(row + k, n_row)}).start()
    wait_bytes(recv_c.at[0 : n_row - 1], recv_sem.at[2])
    gathered = recv_c[...].astype(F32)
    left = jnp.concatenate(
        [
            jnp.concatenate(
                [gathered[r, j * rows : (j + 1) * rows] for r in range(n_row)], axis=0
            )
            for j in range(per)
        ],
        axis=1,
    ).astype(BF16)

    wo_copy.wait()
    for turn in (3, 2, 1, 0):
        first = other_plane(turn) * quarter
        columns = pl.ds(pl.multiple_of(first * HD, quarter * HD), quarter * HD)
        product = jnp.dot(left, wo[:, columns], preferred_element_type=F32).astype(BF16)
        for i in range(quarter):
            send_d[first + i] = product[:, i * HD : (i + 1) * HD]

        def send_sums(i, carry, first=first):
            there = first + lax.rem(place + i, quarter)
            remote(send_d.at[there], recv_d.at[ahead(there) - 1], 3, {"tp": there}).start()
            return carry

        lax.fori_loop(0 if turn else 1, quarter, send_sums, 0)

    recv_d[n_tp - 1] = send_d[me]

    def id_column(base, count, shape, start, column):
        for i in range(count):
            column = jnp.where(iota(shape, 0) == start + i, ids[base + i], column)
        return column

    micro_ids = id_column(
        grp * micro_rows, micro_rows, (micro_rows, HD), 0, jnp.zeros((micro_rows, HD), jnp.int32)
    )
    lane_adapter = lax.div(iota((micro_rows, HD), 1), RANK)
    half_adapters = expand.shape[1] // RANK
    picked = rows * RANK
    group_row = iota((rows, HD), 0)
    group_lane = iota((rows, HD), 1)
    chunks = expand.shape[2] // HD
    stack = recv_f.shape[1] // rows
    tiles = recv_f.shape[0]
    early = chunks // stack
    keep = lax.div(group_lane, RANK) == group_row
    wanted = jnp.zeros((2 * picked, HD), jnp.int32)
    pick_row = iota((2 * picked, HD), 0)
    for half in range(2):
        of_grp = 1 - grp if half == 0 else grp
        for i in range(rows):
            wanted = jnp.where(
                lax.div(pick_row, RANK) == half * rows + i,
                ids[of_grp * micro_rows + row * rows + i],
                wanted,
            )
    wanted = (wanted - grp * half_adapters) * RANK + lax.rem(pick_row, RANK)
    pick_lane = iota((2 * picked, HD), 1)
    pick = jnp.concatenate(
        [
            jnp.where(pick_lane + c * HD == wanted, 1.0, 0.0)
            for c in range(half_adapters * RANK // HD)
        ],
        axis=1,
    ).astype(BF16)
    for copy in expand_copies:
        copy.wait()
    for which in range(2):
        chosen_rows[which] = jnp.dot(
            pick, expand[which], preferred_element_type=F32
        ).astype(BF16)

    resid_copy.wait()
    gain_copy.wait()
    for copy in down_copies:
        copy.wait()
    wait_bytes(recv_d.at[0 : n_tp - 1], recv_sem.at[3])
    hidden = resid[...].astype(F32)
    projected = recv_d[0].astype(F32)
    for s in range(1, n_tp):
        projected += recv_d[s].astype(F32)
    hidden = hidden + projected
    stream_out[...] = hidden.astype(BF16)
    squares = jnp.sum(hidden * hidden, axis=1, keepdims=True)
    scaled = (hidden * gain[...].astype(F32).reshape(1, HD)).astype(BF16)

    def selected(table):
        product = jnp.dot(scaled, table, preferred_element_type=F32)
        per_chunk = HD // RANK
        chosen = jnp.zeros((micro_rows, HD), F32)
        for c in range(product.shape[1] // HD):
            chosen += jnp.where(
                lane_adapter + c * per_chunk == micro_ids, product[:, c * HD : (c + 1) * HD], 0.0
            )
        shift = HD // 2
        while shift >= RANK:
            chosen += pltpu.roll(chosen, shift, 1)
            shift //= 2
        return chosen

    lane = iota((micro_rows, HD), 1)
    own_row = lax.rem(iota((micro_rows, HD), 0), rows)
    ranks = jnp.where(
        lax.rem(lax.div(lane, RANK), 2) == 0, selected(down[0]), selected(down[1])
    )
    ranks = jnp.where(lax.div(lane, 2 * RANK) == own_row, ranks, 0.0)
    squares = jnp.where(lane == own_row, squares, 0.0)

    for r in range(n_row):
        of_group = slice(r * rows, (r + 1) * rows)
        send_e[r, 0:1] = jnp.sum(ranks[of_group], axis=0, keepdims=True)
        send_e[r, 1:2] = jnp.sum(squares[of_group], axis=0, keepdims=True)
    n_first = n_row * n_x
    for dr in range(n_row):
        there = lax.rem(row + dr, n_row)
        for dx in range(n_x):
            if dr or dx:
                remote(
                    send_e.at[there],
                    recv_e.at[dr * n_x + dx - 1],
                    4,
                    {"row": there, "tp": same_plane(dx)},
                ).start()
    recv_e[n_first - 1] = send_e[row]
    wait_bytes(recv_e.at[0 : n_first - 1], recv_sem.at[4])
    summed = recv_e[0]
    for s in range(1, n_first):
        summed += recv_e[s]

    recv_g[n_near - 1] = summed
    mine = recv_g.at[n_near - 1]
    for i in range(n_near):
        remote(mine, recv_g.at[n_near + i], 6, {"grp": 1 - grp, "tp": same_column(i)}).start()
    for i in range(1, n_near):
        remote(mine, recv_g.at[i - 1], 5, {"tp": same_column(i)}).start()

    def expanded(half, first_slot):
        sums = recv_g[first_slot]
        for s in range(1, n_near):
            sums += recv_g[first_slot + s]
        norms = jnp.sum(
            jnp.where(group_lane == group_row, jnp.broadcast_to(sums[1:2], (rows, HD)), 0.0),
            axis=1,
            keepdims=True,
        )
        inverse = lax.rsqrt(norms / (n_row * n_tp * HD) + EPSILON)
        ranks = jnp.broadcast_to(sums[0:1], (rows, HD)) * inverse
        for which in range(2):
            spread_rank = jnp.where(
                lax.div(group_lane, RANK) == 2 * group_row + which, ranks, 0.0
            )
            shift = RANK
            while shift < HD:
                spread_rank += pltpu.roll(spread_rank, shift, 1)
                shift *= 2
            coefficient = jnp.where(keep, spread_rank, 0.0)[:, :picked]
            yield jnp.dot(
                coefficient.astype(BF16),
                chosen_rows[which, half * picked : (half + 1) * picked],
                preferred_element_type=F32,
            )

    wait_bytes(recv_g.at[n_near : 2 * n_near], recv_sem.at[6])
    pieces = []
    for which, delta in enumerate(expanded(0, n_near)):
        pieces += [delta[:, c * HD : (c + 1) * HD] for c in range(chunks)]
        if which:
            pieces += [jnp.zeros((rows, HD), F32)] * (-len(pieces) % stack)
        span = (early, tiles) if which else (0, early)
        for i in range(*span):
            send_f[i] = jnp.concatenate(pieces[i * stack : (i + 1) * stack], axis=0).astype(BF16)
        remote(
            send_f.at[span[0] : span[1]], recv_f.at[span[0] : span[1]], 7 + which, {"grp": 1 - grp}
        ).start()

    wait_bytes(recv_g.at[0 : n_near - 1], recv_sem.at[5])
    own = [delta.astype(BF16).astype(F32) for delta in expanded(1, 0)]
    outs = (gate_out, up_out)
    for which in range(2):
        for c in range(chunks):
            at = which * chunks + c
            if at == 0:
                wait_bytes(recv_f.at[0:early], recv_sem.at[7])
            if at == early * stack:
                wait_bytes(recv_f.at[early:tiles], recv_sem.at[8])
            other = recv_f[at // stack].astype(F32)[at % stack * rows : (at % stack + 1) * rows]
            columns = slice(c * HD, (c + 1) * HD)
            outs[which][:, columns] = (own[which][:, columns] + other).astype(BF16)

    wait_bytes(recv_b.at[0 : n_tp - 1], send_sem.at[0])
    wait_bytes(recv_st.at[0 : n_tp - 1], send_sem.at[1])
    wait_bytes(recv_c.at[0 : n_row - 1], send_sem.at[2])
    wait_bytes(recv_d.at[0 : n_tp - 1], send_sem.at[3])
    wait_bytes(recv_e.at[0 : n_first - 1], send_sem.at[4])
    wait_bytes(recv_g.at[0 : n_near - 1], send_sem.at[5])
    wait_bytes(recv_g.at[n_near : 2 * n_near], send_sem.at[6])
    wait_bytes(send_f.at[0:early], send_sem.at[7])
    wait_bytes(send_f.at[early:tiles], send_sem.at[8])


def hand_over(stream, gate, up, stream_out, gate_out, up_out, sem):
    copies = [
        pltpu.make_async_copy(source, target, sem.at[i])
        for i, (source, target) in enumerate(((stream, stream_out), (gate, gate_out), (up, up_out)))
    ]
    for copy in copies:
        copy.start()
    for copy in copies:
        copy.wait()


def layer(
    sizes,
    query,
    cached_key_rows,
    cached_value_rows,
    row_cache_length,
    attention_output_weight,
    resid,
    feed_norm_scale,
    gate_down_weight,
    up_down_weight,
    gate_expansion_weight,
    up_expansion_weight,
    row_adapter_index,
):
    n_grp, n_row, n_tp = sizes
    rows = query.shape[0]
    heads = query.shape[1] // HD
    tile = rows * (heads // n_tp)
    columns = gate_expansion_weight.shape[1]
    n_core = min(2, n_tp // 4)
    n_x = n_tp // 4 // n_core
    stack = 16 // rows
    packed = -(-2 * (columns // HD) // stack)
    smem = pl.BlockSpec(memory_space=pltpu.SMEM)
    hbm = pl.BlockSpec(memory_space=pl.ANY)
    vmem = pl.BlockSpec(memory_space=pltpu.VMEM)
    parts = pl.pallas_call(
        functools.partial(kernel, sizes),
        out_shape=(
            pltpu.VMEM(resid.shape, BF16),
            pltpu.VMEM((rows, columns), BF16),
            pltpu.VMEM((rows, columns), BF16),
        ),
        in_specs=[smem] * 2 + [hbm] * 10,
        out_specs=(vmem,) * 3,
        scratch_shapes=[
            pltpu.VMEM(query.shape, BF16),
            pltpu.VMEM(cached_key_rows.shape, BF16),
            pltpu.VMEM(cached_value_rows.shape, BF16),
            pltpu.VMEM(attention_output_weight.shape, BF16),
            pltpu.VMEM(resid.shape, BF16),
            pltpu.VMEM(feed_norm_scale.shape, BF16),
            pltpu.VMEM((2,) + gate_down_weight.shape, BF16),
            pltpu.VMEM((2,) + gate_expansion_weight.shape, BF16),
            pltpu.VMEM((rows, heads, cached_key_rows.shape[1]), BF16),
            pltpu.VMEM((rows, heads, HD), F32),
            pltpu.VMEM((n_tp, tile, HD), F32),
            pltpu.VMEM((heads, HD), F32),
            pltpu.VMEM((n_tp * tile, HD), F32),
            pltpu.VMEM((n_tp, tile, HD), BF16),
            pltpu.VMEM((n_tp, 1, HD), F32),
            pltpu.VMEM((n_tp, tile, HD), BF16),
            pltpu.VMEM((n_tp, 1, HD), F32),
            pltpu.VMEM((n_row, tile, HD), BF16),
            pltpu.VMEM((n_tp, n_row * rows, HD), BF16),
            pltpu.VMEM((n_tp, n_row * rows, HD), BF16),
            pltpu.VMEM((n_row, 2, HD), F32),
            pltpu.VMEM((n_row * n_x, 2, HD), F32),
            pltpu.VMEM((8 * n_core, 2, HD), F32),
            pltpu.VMEM((packed, 16, HD), BF16),
            pltpu.VMEM((packed, 16, HD), BF16),
            pltpu.VMEM((2, 2 * rows * RANK, columns), BF16),
            pltpu.SemaphoreType.DMA((8,)),
            pltpu.SemaphoreType.DMA((2, rows)),
            pltpu.SemaphoreType.DMA((9,)),
            pltpu.SemaphoreType.DMA((9,)),
        ],
        compiler_params=pltpu.CompilerParams(
            collective_id=0, has_side_effects=True, vmem_limit_bytes=56 * 1024 * 1024
        ),
    )(
        row_cache_length,
        row_adapter_index,
        query,
        cached_key_rows,
        cached_value_rows,
        attention_output_weight,
        resid,
        feed_norm_scale,
        gate_down_weight,
        up_down_weight,
        gate_expansion_weight,
        up_expansion_weight,
    )
    return pl.pallas_call(
        hand_over,
        out_shape=tuple(jax.ShapeDtypeStruct(part.shape, part.dtype) for part in parts),
        in_specs=[hbm] * 3,
        out_specs=(pl.BlockSpec(memory_space=pltpu.HBM),) * 3,
        scratch_shapes=[pltpu.SemaphoreType.DMA((3,))],
            compiler_params=pltpu.CompilerParams(vmem_limit_bytes=1024 * 1024),
    )(*[pltpu.with_memory_space_constraint(p, pltpu.VMEM) for p in parts])


def solution(mesh):
    sizes = tuple(mesh.shape[axis] for axis in ("grp", "row", "tp"))
    return jax.shard_map(
        functools.partial(layer, sizes),
        mesh=mesh,
        in_specs=(
            P(("grp", "row"), None),
            P(("grp", "row"), "tp", None),
            P(("grp", "row"), "tp", None),
            P(("grp", "row")),
            P("tp", "row"),
            P("grp", ("row", "tp")),
            P(("row", "tp")),
            P(("row", "tp"), None),
            P(("row", "tp"), None),
            P("grp", "tp"),
            P("grp", "tp"),
            P(),
        ),
        out_specs=(P("grp", ("row", "tp")), P(("grp", "row"), "tp"), P(("grp", "row"), "tp")),
        check_vma=False,
    )
```

```python
import functools

import jax
import jax.numpy as jnp
from jax import lax
from jax.experimental import pallas as pl
from jax.experimental.pallas import tpu as pltpu
from jax.sharding import PartitionSpec as P

HD = 128
RANK = 16
EPSILON = 1e-05
MESH = pl.DeviceIdType.MESH
F32 = jnp.float32
BF16 = jnp.bfloat16


def iota(shape, axis):
    return lax.broadcasted_iota(jnp.int32, shape, axis)


def kernel(
    sizes,
    lengths,
    ids,
    query_hbm,
    key_hbm,
    value_hbm,
    wo_hbm,
    resid_hbm,
    gain_hbm,
    gate_down_hbm,
    up_down_hbm,
    gate_exp_hbm,
    up_exp_hbm,
    stream_out,
    gate_out,
    up_out,
    query,
    keys,
    values,
    wo,
    resid,
    gain,
    down,
    expand,
    weights_s,
    acc_s,
    share_s,
    stat_s,
    msg_s,
    send_b,
    send_st,
    recv_b,
    recv_st,
    recv_c,
    send_d,
    recv_d,
    send_e,
    recv_e,
    recv_g,
    send_f,
    recv_f,
    chosen_rows,
    load_sem,
    kv_sem,
    send_sem,
    recv_sem,
    answer,
):
    n_grp, n_row, n_tp = sizes
    rows, positions, kv_width = keys.shape
    kv_heads = kv_width // HD
    heads = query.shape[1] // HD
    group = heads // kv_heads
    per = heads // n_tp
    tile = rows * per
    micro_rows = n_row * rows
    grp = lax.axis_index("grp")
    row = lax.axis_index("row")
    me = lax.axis_index("tp")

    def load(source, target, index):
        copy = pltpu.make_async_copy(source, target, load_sem.at[index])
        copy.start()
        return copy

    def wait_bytes(ref, sem):
        pltpu.make_async_copy(ref, ref, sem).wait()

    quarter = n_tp // 4
    plane = lax.div(me, quarter)
    place = lax.rem(me, quarter)
    n_core = min(2, quarter)
    n_x = quarter // n_core
    place_x = lax.div(place, n_core)
    core = lax.rem(place, n_core)
    n_near = 4 * n_core

    def other_plane(turn):
        high = lax.rem(lax.div(plane, 2) + turn // 2, 2)
        return 2 * high + lax.rem(plane + turn % 2, 2)

    def ahead(there):
        return lax.rem(there - me + n_tp, n_tp)

    query_copy = load(query_hbm, query, 0)
    key_copies = [
        pltpu.make_async_copy(key_hbm.at[b], keys.at[b], kv_sem.at[0, b]) for b in range(rows)
    ]
    value_copies = [
        pltpu.make_async_copy(value_hbm.at[b], values.at[b], kv_sem.at[1, b]) for b in range(rows)
    ]
    in_order = key_copies + value_copies
    flying = rows + rows // 2
    for copy in in_order[:flying]:
        copy.start()

    def arrived(first, count):
        for i in range(first, first + count):
            in_order[i].wait()
            if i + flying < 2 * rows:
                in_order[i + flying].start()

    barrier = pltpu.get_barrier_semaphore()

    def same_plane(dx):
        return plane * quarter + lax.rem(place_x + dx, n_x) * n_core + core

    def same_column(i):
        there = lax.rem(plane + i // n_core, 4) * quarter + place_x * n_core
        return there + lax.rem(core + i % n_core, n_core)

    def greet(k, carry):
        there = lax.rem(me + k, n_tp)
        pl.semaphore_signal(barrier, inc=1, device_id={"tp": there}, device_id_type=MESH)
        return carry

    @pl.when(grp == 0)
    def _():
        for i in range(n_near):
            pl.semaphore_signal(
                barrier,
                inc=1,
                device_id={"grp": 1 - grp, "tp": same_column(i)},
                device_id_type=MESH,
            )

    lax.fori_loop(1, n_tp, greet, 0)
    for dr in range(1, n_row):
        for dx in range(n_x):
            pl.semaphore_signal(
                barrier,
                inc=1,
                device_id={"row": lax.rem(row + dr, n_row), "tp": same_plane(dx)},
                device_id_type=MESH,
            )

    query_copy.wait()
    head_rows = query[...].astype(F32).reshape(rows, heads, HD).astype(BF16)
    position = me * positions + iota((heads, positions), 1)
    stat_lane = iota((heads, HD), 1) - rows * lax.rem(iota((heads, HD), 0), per)
    stats = jnp.zeros((heads, HD), F32)
    arrived(0, rows)
    for b in range(rows):
        scores = jnp.concatenate(
            [
                lax.dot_general(
                    head_rows[b, k * group : (k + 1) * group],
                    keys[b, :, k * HD : (k + 1) * HD],
                    (((1,), (1,)), ((), ())),
                    preferred_element_type=F32,
                )
                for k in range(kv_heads)
            ],
            axis=0,
        ) * (HD ** (-0.5))
        visible = position < lengths[b]
        masked = jnp.where(visible, scores, -1e30)
        highest = jnp.max(masked, axis=1, keepdims=True)
        weights = jnp.where(visible, jnp.exp(masked - highest), 0.0)
        total = jnp.sum(weights, axis=1, keepdims=True)
        weights_s[b] = weights.astype(BF16)
        stats = jnp.where(stat_lane == b, highest, stats)
        stats = jnp.where(stat_lane == tile + b, total, stats)
    stat_s[...] = stats
    stat_rows = stat_s[pl.ds(0, n_tp, stride=per), :]
    for j in range(1, per):
        stat_rows += stat_s[pl.ds(j, n_tp, stride=per), :]
    send_st[...] = stat_rows.reshape(n_tp, 1, HD)

    within = n_tp - 1 + (n_row - 1) * n_x

    @pl.when(grp == 0)
    def _():
        pl.semaphore_wait(barrier, within)

    @pl.when(grp == 1)
    def _():
        pl.semaphore_wait(barrier, within + n_near)
        for i in range(n_near):
            pl.semaphore_signal(
                answer,
                inc=1,
                device_id={"grp": 1 - grp, "tp": same_column(i)},
                device_id_type=MESH,
            )

    def remote(source, target, index, device):
        return pltpu.make_async_remote_copy(
            src_ref=source,
            dst_ref=target,
            send_sem=send_sem.at[index],
            recv_sem=recv_sem.at[index],
            device_id=device,
            device_id_type=MESH,
        )

    def send_stats(k, carry):
        there = lax.rem(me + k, n_tp)
        remote(send_st.at[there], recv_st.at[k - 1], 1, {"tp": there}).start()
        return carry

    lax.fori_loop(1, n_tp, send_stats, 0)
    recv_st[n_tp - 1] = send_st[me]
    wo_copy = load(wo_hbm, wo, 1)
    resid_copy = load(resid_hbm, resid, 2)
    gain_copy = load(gain_hbm, gain, 3)
    down_copies = (load(gate_down_hbm, down.at[0], 4), load(up_down_hbm, down.at[1], 5))
    expand_copies = (load(gate_exp_hbm, expand.at[0], 6), load(up_exp_hbm, expand.at[1], 7))

    for b in range(rows):
        if b % 2 == 0:
            arrived(rows + b, 2)
        weights = weights_s[b]
        for k in range(kv_heads):
            acc_s[b, k * group : (k + 1) * group, :] = jnp.dot(
                weights[k * group : (k + 1) * group],
                values[b, :, k * HD : (k + 1) * HD],
                preferred_element_type=F32,
            )
        for j in range(per):
            msg_s[pl.ds(j * rows + b, n_tp, stride=tile), :] = acc_s[
                b, pl.ds(j, n_tp, stride=per), :
            ]
    send_b[...] = msg_s[...].reshape(n_tp, tile, HD).astype(BF16)

    def send_partial(k, carry):
        there = lax.rem(me + k, n_tp)
        remote(send_b.at[there], recv_b.at[k - 1], 0, {"tp": there}).start()
        return carry

    lax.fori_loop(1, n_tp, send_partial, 0)
    recv_b[n_tp - 1] = send_b[me]

    wait_bytes(recv_st.at[0 : n_tp - 1], recv_sem.at[1])
    part_stats = recv_st[...].reshape(n_tp, HD)
    overall = jnp.max(part_stats, axis=0, keepdims=True)
    factor = jnp.exp(part_stats - overall)
    part_totals = pltpu.roll(part_stats, HD - tile, 1)
    normal = jnp.sum(factor * part_totals, axis=0, keepdims=True)
    share = jnp.where(iota((n_tp, HD), 1) < tile, factor / normal, 0.0)
    share = share.T[:tile]
    for s in range(n_tp):
        share_s[s] = jnp.broadcast_to(share[:, s : s + 1], (tile, HD))
    wait_bytes(recv_b.at[0 : n_tp - 1], recv_sem.at[0])
    attended = share_s[0] * recv_b[0].astype(F32)
    for s in range(1, n_tp):
        attended += share_s[s] * recv_b[s].astype(F32)

    recv_c[row] = attended.astype(BF16)
    for k in range(1, n_row):
        remote(recv_c.at[row], recv_c.at[row], 2, {"row": lax.rem(row + k, n_row)}).start()
    wait_bytes(recv_c.at[0 : n_row - 1], recv_sem.at[2])
    gathered = recv_c[...].astype(F32)
    left = jnp.concatenate(
        [
            jnp.concatenate(
                [gathered[r, j * rows : (j + 1) * rows] for r in range(n_row)], axis=0
            )
            for j in range(per)
        ],
        axis=1,
    ).astype(BF16)

    wo_copy.wait()
    for turn in (3, 2, 1, 0):
        first = other_plane(turn) * quarter
        columns = pl.ds(pl.multiple_of(first * HD, quarter * HD), quarter * HD)
        product = jnp.dot(left, wo[:, columns], preferred_element_type=F32).astype(BF16)
        for i in range(quarter):
            send_d[first + i] = product[:, i * HD : (i + 1) * HD]

        def send_sums(i, carry, first=first):
            there = first + lax.rem(place + i, quarter)
            remote(send_d.at[there], recv_d.at[ahead(there) - 1], 3, {"tp": there}).start()
            return carry

        lax.fori_loop(0 if turn else 1, quarter, send_sums, 0)

    recv_d[n_tp - 1] = send_d[me]

    def id_column(base, count, shape, start, column):
        for i in range(count):
            column = jnp.where(iota(shape, 0) == start + i, ids[base + i], column)
        return column

    micro_ids = id_column(
        grp * micro_rows, micro_rows, (micro_rows, HD), 0, jnp.zeros((micro_rows, HD), jnp.int32)
    )
    lane_adapter = lax.div(iota((micro_rows, HD), 1), RANK)
    half_adapters = expand.shape[1] // RANK
    picked = rows * RANK
    group_row = iota((rows, HD), 0)
    group_lane = iota((rows, HD), 1)
    chunks = expand.shape[2] // HD
    stack = recv_f.shape[1] // rows
    tiles = recv_f.shape[0]
    early = chunks // stack
    keep = lax.div(group_lane, RANK) == group_row
    wanted = jnp.zeros((2 * picked, HD), jnp.int32)
    pick_row = iota((2 * picked, HD), 0)
    for half in range(2):
        of_grp = 1 - grp if half == 0 else grp
        for i in range(rows):
            wanted = jnp.where(
                lax.div(pick_row, RANK) == half * rows + i,
                ids[of_grp * micro_rows + row * rows + i],
                wanted,
            )
    wanted = (wanted - grp * half_adapters) * RANK + lax.rem(pick_row, RANK)
    pick_lane = iota((2 * picked, HD), 1)
    pick = jnp.concatenate(
        [
            jnp.where(pick_lane + c * HD == wanted, 1.0, 0.0)
            for c in range(half_adapters * RANK // HD)
        ],
        axis=1,
    ).astype(BF16)
    for copy in expand_copies:
        copy.wait()
    for which in range(2):
        chosen_rows[which] = jnp.dot(
            pick, expand[which], preferred_element_type=F32
        ).astype(BF16)

    resid_copy.wait()
    gain_copy.wait()
    for copy in down_copies:
        copy.wait()
    wait_bytes(recv_d.at[0 : n_tp - 1], recv_sem.at[3])
    hidden = resid[...].astype(F32)
    projected = recv_d[0].astype(F32)
    for s in range(1, n_tp):
        projected += recv_d[s].astype(F32)
    hidden = hidden + projected
    stream_out[...] = hidden.astype(BF16)
    squares = jnp.sum(hidden * hidden, axis=1, keepdims=True)
    scaled = (hidden * gain[...].astype(F32).reshape(1, HD)).astype(BF16)

    def selected(table):
        product = jnp.dot(scaled, table, preferred_element_type=F32)
        per_chunk = HD // RANK
        chosen = jnp.zeros((micro_rows, HD), F32)
        for c in range(product.shape[1] // HD):
            chosen += jnp.where(
                lane_adapter + c * per_chunk == micro_ids, product[:, c * HD : (c + 1) * HD], 0.0
            )
        shift = HD // 2
        while shift >= RANK:
            chosen += pltpu.roll(chosen, shift, 1)
            shift //= 2
        return chosen

    lane = iota((micro_rows, HD), 1)
    own_row = lax.rem(iota((micro_rows, HD), 0), rows)
    ranks = jnp.where(
        lax.rem(lax.div(lane, RANK), 2) == 0, selected(down[0]), selected(down[1])
    )
    ranks = jnp.where(lax.div(lane, 2 * RANK) == own_row, ranks, 0.0)
    squares = jnp.where(lane == own_row, squares, 0.0)

    for r in range(n_row):
        of_group = slice(r * rows, (r + 1) * rows)
        send_e[r, 0:1] = jnp.sum(ranks[of_group], axis=0, keepdims=True)
        send_e[r, 1:2] = jnp.sum(squares[of_group], axis=0, keepdims=True)
    n_first = n_row * n_x
    for dr in range(n_row):
        there = lax.rem(row + dr, n_row)
        for dx in range(n_x):
            if dr or dx:
                remote(
                    send_e.at[there],
                    recv_e.at[dr * n_x + dx - 1],
                    4,
                    {"row": there, "tp": same_plane(dx)},
                ).start()
    recv_e[n_first - 1] = send_e[row]
    wait_bytes(recv_e.at[0 : n_first - 1], recv_sem.at[4])
    summed = recv_e[0]
    for s in range(1, n_first):
        summed += recv_e[s]

    recv_g[n_near - 1] = summed
    mine = recv_g.at[n_near - 1]

    @pl.when(grp == 0)
    def _():
        pl.semaphore_wait(answer, n_near)

    for i in range(n_near):
        remote(mine, recv_g.at[n_near + i], 6, {"grp": 1 - grp, "tp": same_column(i)}).start()
    for i in range(1, n_near):
        remote(mine, recv_g.at[i - 1], 5, {"tp": same_column(i)}).start()

    def expanded(half, first_slot):
        sums = recv_g[first_slot]
        for s in range(1, n_near):
            sums += recv_g[first_slot + s]
        norms = jnp.sum(
            jnp.where(group_lane == group_row, jnp.broadcast_to(sums[1:2], (rows, HD)), 0.0),
            axis=1,
            keepdims=True,
        )
        inverse = lax.rsqrt(norms / (n_row * n_tp * HD) + EPSILON)
        ranks = jnp.broadcast_to(sums[0:1], (rows, HD)) * inverse
        for which in range(2):
            spread_rank = jnp.where(
                lax.div(group_lane, RANK) == 2 * group_row + which, ranks, 0.0
            )
            shift = RANK
            while shift < HD:
                spread_rank += pltpu.roll(spread_rank, shift, 1)
                shift *= 2
            coefficient = jnp.where(keep, spread_rank, 0.0)[:, :picked]
            yield jnp.dot(
                coefficient.astype(BF16),
                chosen_rows[which, half * picked : (half + 1) * picked],
                preferred_element_type=F32,
            )

    wait_bytes(recv_g.at[n_near : 2 * n_near], recv_sem.at[6])
    pieces = []
    for which, delta in enumerate(expanded(0, n_near)):
        pieces += [delta[:, c * HD : (c + 1) * HD] for c in range(chunks)]
        if which:
            pieces += [jnp.zeros((rows, HD), F32)] * (-len(pieces) % stack)
        span = (early, tiles) if which else (0, early)
        for i in range(*span):
            send_f[i] = jnp.concatenate(pieces[i * stack : (i + 1) * stack], axis=0).astype(BF16)
        remote(
            send_f.at[span[0] : span[1]], recv_f.at[span[0] : span[1]], 7 + which, {"grp": 1 - grp}
        ).start()

    wait_bytes(recv_g.at[0 : n_near - 1], recv_sem.at[5])
    own = [delta.astype(BF16).astype(F32) for delta in expanded(1, 0)]
    outs = (gate_out, up_out)
    for which in range(2):
        for c in range(chunks):
            at = which * chunks + c
            if at == 0:
                wait_bytes(recv_f.at[0:early], recv_sem.at[7])
            if at == early * stack:
                wait_bytes(recv_f.at[early:tiles], recv_sem.at[8])
            other = recv_f[at // stack].astype(F32)[at % stack * rows : (at % stack + 1) * rows]
            columns = slice(c * HD, (c + 1) * HD)
            outs[which][:, columns] = (own[which][:, columns] + other).astype(BF16)

    wait_bytes(recv_b.at[0 : n_tp - 1], send_sem.at[0])
    wait_bytes(recv_st.at[0 : n_tp - 1], send_sem.at[1])
    wait_bytes(recv_c.at[0 : n_row - 1], send_sem.at[2])
    wait_bytes(recv_d.at[0 : n_tp - 1], send_sem.at[3])
    wait_bytes(recv_e.at[0 : n_first - 1], send_sem.at[4])
    wait_bytes(recv_g.at[0 : n_near - 1], send_sem.at[5])
    wait_bytes(recv_g.at[n_near : 2 * n_near], send_sem.at[6])
    wait_bytes(send_f.at[0:early], send_sem.at[7])
    wait_bytes(send_f.at[early:tiles], send_sem.at[8])


def hand_over(stream, gate, up, stream_out, gate_out, up_out, sem):
    copies = [
        pltpu.make_async_copy(source, target, sem.at[i])
        for i, (source, target) in enumerate(((stream, stream_out), (gate, gate_out), (up, up_out)))
    ]
    for copy in copies:
        copy.start()
    for copy in copies:
        copy.wait()


def layer(
    sizes,
    query,
    cached_key_rows,
    cached_value_rows,
    row_cache_length,
    attention_output_weight,
    resid,
    feed_norm_scale,
    gate_down_weight,
    up_down_weight,
    gate_expansion_weight,
    up_expansion_weight,
    row_adapter_index,
):
    n_grp, n_row, n_tp = sizes
    rows = query.shape[0]
    heads = query.shape[1] // HD
    tile = rows * (heads // n_tp)
    columns = gate_expansion_weight.shape[1]
    n_core = min(2, n_tp // 4)
    n_x = n_tp // 4 // n_core
    stack = 16 // rows
    packed = -(-2 * (columns // HD) // stack)
    smem = pl.BlockSpec(memory_space=pltpu.SMEM)
    hbm = pl.BlockSpec(memory_space=pl.ANY)
    vmem = pl.BlockSpec(memory_space=pltpu.VMEM)
    parts = pl.pallas_call(
        functools.partial(kernel, sizes),
        out_shape=(
            pltpu.VMEM(resid.shape, BF16),
            pltpu.VMEM((rows, columns), BF16),
            pltpu.VMEM((rows, columns), BF16),
        ),
        in_specs=[smem] * 2 + [hbm] * 10,
        out_specs=(vmem,) * 3,
        scratch_shapes=[
            pltpu.VMEM(query.shape, BF16),
            pltpu.VMEM(cached_key_rows.shape, BF16),
            pltpu.VMEM(cached_value_rows.shape, BF16),
            pltpu.VMEM(attention_output_weight.shape, BF16),
            pltpu.VMEM(resid.shape, BF16),
            pltpu.VMEM(feed_norm_scale.shape, BF16),
            pltpu.VMEM((2,) + gate_down_weight.shape, BF16),
            pltpu.VMEM((2,) + gate_expansion_weight.shape, BF16),
            pltpu.VMEM((rows, heads, cached_key_rows.shape[1]), BF16),
            pltpu.VMEM((rows, heads, HD), F32),
            pltpu.VMEM((n_tp, tile, HD), F32),
            pltpu.VMEM((heads, HD), F32),
            pltpu.VMEM((n_tp * tile, HD), F32),
            pltpu.VMEM((n_tp, tile, HD), BF16),
            pltpu.VMEM((n_tp, 1, HD), F32),
            pltpu.VMEM((n_tp, tile, HD), BF16),
            pltpu.VMEM((n_tp, 1, HD), F32),
            pltpu.VMEM((n_row, tile, HD), BF16),
            pltpu.VMEM((n_tp, n_row * rows, HD), BF16),
            pltpu.VMEM((n_tp, n_row * rows, HD), BF16),
            pltpu.VMEM((n_row, 2, HD), F32),
            pltpu.VMEM((n_row * n_x, 2, HD), F32),
            pltpu.VMEM((8 * n_core, 2, HD), F32),
            pltpu.VMEM((packed, 16, HD), BF16),
            pltpu.VMEM((packed, 16, HD), BF16),
            pltpu.VMEM((2, 2 * rows * RANK, columns), BF16),
            pltpu.SemaphoreType.DMA((8,)),
            pltpu.SemaphoreType.DMA((2, rows)),
            pltpu.SemaphoreType.DMA((9,)),
            pltpu.SemaphoreType.DMA((9,)),
            pltpu.SemaphoreType.REGULAR,
        ],
        compiler_params=pltpu.CompilerParams(
            collective_id=0, has_side_effects=True, vmem_limit_bytes=56 * 1024 * 1024
        ),
    )(
        row_cache_length,
        row_adapter_index,
        query,
        cached_key_rows,
        cached_value_rows,
        attention_output_weight,
        resid,
        feed_norm_scale,
        gate_down_weight,
        up_down_weight,
        gate_expansion_weight,
        up_expansion_weight,
    )
    return pl.pallas_call(
        hand_over,
        out_shape=tuple(jax.ShapeDtypeStruct(part.shape, part.dtype) for part in parts),
        in_specs=[hbm] * 3,
        out_specs=(pl.BlockSpec(memory_space=pltpu.HBM),) * 3,
        scratch_shapes=[pltpu.SemaphoreType.DMA((3,))],
            compiler_params=pltpu.CompilerParams(vmem_limit_bytes=1024 * 1024),
    )(*[pltpu.with_memory_space_constraint(p, pltpu.VMEM) for p in parts])


def solution(mesh):
    sizes = tuple(mesh.shape[axis] for axis in ("grp", "row", "tp"))
    return jax.shard_map(
        functools.partial(layer, sizes),
        mesh=mesh,
        in_specs=(
            P(("grp", "row"), None),
            P(("grp", "row"), "tp", None),
            P(("grp", "row"), "tp", None),
            P(("grp", "row")),
            P("tp", "row"),
            P("grp", ("row", "tp")),
            P(("row", "tp")),
            P(("row", "tp"), None),
            P(("row", "tp"), None),
            P("grp", "tp"),
            P("grp", "tp"),
            P(),
        ),
        out_specs=(P("grp", ("row", "tp")), P(("grp", "row"), "tp"), P(("grp", "row"), "tp")),
        check_vma=False,
    )
```

```python
import functools

import jax
import jax.numpy as jnp
from jax import lax
from jax.experimental import pallas as pl
from jax.experimental.pallas import tpu as pltpu
from jax.sharding import PartitionSpec as P

HD = 128
RANK = 16
EPSILON = 1e-05
MESH = pl.DeviceIdType.MESH
F32 = jnp.float32
BF16 = jnp.bfloat16


def iota(shape, axis):
    return lax.broadcasted_iota(jnp.int32, shape, axis)


def kernel(
    sizes,
    lengths_hbm,
    ids_hbm,
    query_hbm,
    key_hbm,
    value_hbm,
    wo_hbm,
    resid_hbm,
    gain_hbm,
    gate_down_hbm,
    up_down_hbm,
    gate_exp_hbm,
    up_exp_hbm,
    stream_out,
    gate_out,
    up_out,
    lengths,
    ids,
    query,
    keys,
    values,
    wo,
    resid,
    gain,
    down,
    expand,
    weights_s,
    acc_s,
    share_s,
    stat_s,
    msg_s,
    send_b,
    send_st,
    recv_b,
    recv_st,
    recv_c,
    send_d,
    recv_d,
    send_e,
    recv_e,
    recv_g,
    send_f,
    recv_f,
    chosen_rows,
    load_sem,
    kv_sem,
    send_sem,
    recv_sem,
    answer,
):
    n_grp, n_row, n_tp = sizes
    rows, positions, kv_width = keys.shape
    kv_heads = kv_width // HD
    heads = query.shape[1] // HD
    group = heads // kv_heads
    per = heads // n_tp
    tile = rows * per
    micro_rows = n_row * rows
    grp = lax.axis_index("grp")
    row = lax.axis_index("row")
    me = lax.axis_index("tp")

    def load(source, target, index):
        copy = pltpu.make_async_copy(source, target, load_sem.at[index])
        copy.start()
        return copy

    def wait_bytes(ref, sem):
        pltpu.make_async_copy(ref, ref, sem).wait()

    quarter = n_tp // 4
    plane = lax.div(me, quarter)
    place = lax.rem(me, quarter)
    n_core = min(2, quarter)
    n_x = quarter // n_core
    place_x = lax.div(place, n_core)
    core = lax.rem(place, n_core)
    n_near = 4 * n_core

    def other_plane(turn):
        high = lax.rem(lax.div(plane, 2) + turn // 2, 2)
        return 2 * high + lax.rem(plane + turn % 2, 2)

    def ahead(there):
        return lax.rem(there - me + n_tp, n_tp)

    query_copy = load(query_hbm, query, 0)
    key_copies = [
        pltpu.make_async_copy(key_hbm.at[b], keys.at[b], kv_sem.at[0, b]) for b in range(rows)
    ]
    value_copies = [
        pltpu.make_async_copy(value_hbm.at[b], values.at[b], kv_sem.at[1, b]) for b in range(rows)
    ]
    in_order = key_copies + value_copies
    flying = rows + rows // 2
    for copy in in_order[:flying]:
        copy.start()

    lengths_copy = load(lengths_hbm, lengths, 8)
    ids_copy = load(ids_hbm, ids, 9)

    def arrived(first, count):
        for i in range(first, first + count):
            in_order[i].wait()
            if i + flying < 2 * rows:
                in_order[i + flying].start()

    barrier = pltpu.get_barrier_semaphore()

    def same_plane(dx):
        return plane * quarter + lax.rem(place_x + dx, n_x) * n_core + core

    def same_column(i):
        there = lax.rem(plane + i // n_core, 4) * quarter + place_x * n_core
        return there + lax.rem(core + i % n_core, n_core)

    def greet(k, carry):
        there = lax.rem(me + k, n_tp)
        pl.semaphore_signal(barrier, inc=1, device_id={"tp": there}, device_id_type=MESH)
        return carry

    @pl.when(grp == 0)
    def _():
        for i in range(n_near):
            pl.semaphore_signal(
                barrier,
                inc=1,
                device_id={"grp": 1 - grp, "tp": same_column(i)},
                device_id_type=MESH,
            )

    lax.fori_loop(1, n_tp, greet, 0)
    for dr in range(1, n_row):
        for dx in range(n_x):
            pl.semaphore_signal(
                barrier,
                inc=1,
                device_id={"row": lax.rem(row + dr, n_row), "tp": same_plane(dx)},
                device_id_type=MESH,
            )

    query_copy.wait()
    head_rows = query[...].astype(F32).reshape(rows, heads, HD).astype(BF16)
    position = me * positions + iota((heads, positions), 1)
    stat_lane = iota((heads, HD), 1) - rows * lax.rem(iota((heads, HD), 0), per)
    stats = jnp.zeros((heads, HD), F32)
    lengths_copy.wait()
    arrived(0, rows)
    for b in range(rows):
        scores = jnp.concatenate(
            [
                lax.dot_general(
                    head_rows[b, k * group : (k + 1) * group],
                    keys[b, :, k * HD : (k + 1) * HD],
                    (((1,), (1,)), ((), ())),
                    preferred_element_type=F32,
                )
                for k in range(kv_heads)
            ],
            axis=0,
        ) * (HD ** (-0.5))
        visible = position < lengths[b]
        masked = jnp.where(visible, scores, -1e30)
        highest = jnp.max(masked, axis=1, keepdims=True)
        weights = jnp.where(visible, jnp.exp(masked - highest), 0.0)
        total = jnp.sum(weights, axis=1, keepdims=True)
        weights_s[b] = weights.astype(BF16)
        stats = jnp.where(stat_lane == b, highest, stats)
        stats = jnp.where(stat_lane == tile + b, total, stats)
    stat_s[...] = stats
    stat_rows = stat_s[pl.ds(0, n_tp, stride=per), :]
    for j in range(1, per):
        stat_rows += stat_s[pl.ds(j, n_tp, stride=per), :]
    send_st[...] = stat_rows.reshape(n_tp, 1, HD)

    within = n_tp - 1 + (n_row - 1) * n_x

    @pl.when(grp == 0)
    def _():
        pl.semaphore_wait(barrier, within)

    @pl.when(grp == 1)
    def _():
        pl.semaphore_wait(barrier, within + n_near)
        for i in range(n_near):
            pl.semaphore_signal(
                answer,
                inc=1,
                device_id={"grp": 1 - grp, "tp": same_column(i)},
                device_id_type=MESH,
            )

    def remote(source, target, index, device):
        return pltpu.make_async_remote_copy(
            src_ref=source,
            dst_ref=target,
            send_sem=send_sem.at[index],
            recv_sem=recv_sem.at[index],
            device_id=device,
            device_id_type=MESH,
        )

    def send_stats(k, carry):
        there = lax.rem(me + k, n_tp)
        remote(send_st.at[there], recv_st.at[k - 1], 1, {"tp": there}).start()
        return carry

    lax.fori_loop(1, n_tp, send_stats, 0)
    recv_st[n_tp - 1] = send_st[me]
    wo_copy = load(wo_hbm, wo, 1)
    resid_copy = load(resid_hbm, resid, 2)
    gain_copy = load(gain_hbm, gain, 3)
    down_copies = (load(gate_down_hbm, down.at[0], 4), load(up_down_hbm, down.at[1], 5))
    expand_copies = (load(gate_exp_hbm, expand.at[0], 6), load(up_exp_hbm, expand.at[1], 7))

    for b in range(rows):
        if b % 2 == 0:
            arrived(rows + b, 2)
        weights = weights_s[b]
        for k in range(kv_heads):
            acc_s[b, k * group : (k + 1) * group, :] = jnp.dot(
                weights[k * group : (k + 1) * group],
                values[b, :, k * HD : (k + 1) * HD],
                preferred_element_type=F32,
            )
        for j in range(per):
            msg_s[pl.ds(j * rows + b, n_tp, stride=tile), :] = acc_s[
                b, pl.ds(j, n_tp, stride=per), :
            ]
    send_b[...] = msg_s[...].reshape(n_tp, tile, HD).astype(BF16)

    for turn in (3, 2, 1, 0):

        def send_partial(i, carry, turn=turn):
            there = other_plane(turn) * quarter + lax.rem(place + i, quarter)
            remote(send_b.at[there], recv_b.at[ahead(there) - 1], 0, {"tp": there}).start()
            return carry

        lax.fori_loop(0 if turn else 1, quarter, send_partial, 0)
    recv_b[n_tp - 1] = send_b[me]

    wait_bytes(recv_st.at[0 : n_tp - 1], recv_sem.at[1])
    part_stats = recv_st[...].reshape(n_tp, HD)
    overall = jnp.max(part_stats, axis=0, keepdims=True)
    factor = jnp.exp(part_stats - overall)
    part_totals = pltpu.roll(part_stats, HD - tile, 1)
    normal = jnp.sum(factor * part_totals, axis=0, keepdims=True)
    share = jnp.where(iota((n_tp, HD), 1) < tile, factor / normal, 0.0)
    share = share.T[:tile]
    for s in range(n_tp):
        share_s[s] = jnp.broadcast_to(share[:, s : s + 1], (tile, HD))
    wait_bytes(recv_b.at[0 : n_tp - 1], recv_sem.at[0])
    attended = share_s[0] * recv_b[0].astype(F32)
    for s in range(1, n_tp):
        attended += share_s[s] * recv_b[s].astype(F32)

    recv_c[row] = attended.astype(BF16)
    for k in range(1, n_row):
        remote(recv_c.at[row], recv_c.at[row], 2, {"row": lax.rem(row + k, n_row)}).start()
    wait_bytes(recv_c.at[0 : n_row - 1], recv_sem.at[2])
    gathered = recv_c[...].astype(F32)
    left = jnp.concatenate(
        [
            jnp.concatenate(
                [gathered[r, j * rows : (j + 1) * rows] for r in range(n_row)], axis=0
            )
            for j in range(per)
        ],
        axis=1,
    ).astype(BF16)

    wo_copy.wait()
    for turn in (3, 2, 1, 0):
        first = other_plane(turn) * quarter
        columns = pl.ds(pl.multiple_of(first * HD, quarter * HD), quarter * HD)
        product = jnp.dot(left, wo[:, columns], preferred_element_type=F32).astype(BF16)
        for i in range(quarter):
            send_d[first + i] = product[:, i * HD : (i + 1) * HD]

        def send_sums(i, carry, first=first):
            there = first + lax.rem(place + i, quarter)
            remote(send_d.at[there], recv_d.at[ahead(there) - 1], 3, {"tp": there}).start()
            return carry

        lax.fori_loop(0 if turn else 1, quarter, send_sums, 0)

    recv_d[n_tp - 1] = send_d[me]

    def id_column(base, count, shape, start, column):
        for i in range(count):
            column = jnp.where(iota(shape, 0) == start + i, ids[base + i], column)
        return column

    ids_copy.wait()
    micro_ids = id_column(
        grp * micro_rows, micro_rows, (micro_rows, HD), 0, jnp.zeros((micro_rows, HD), jnp.int32)
    )
    lane_adapter = lax.div(iota((micro_rows, HD), 1), RANK)
    half_adapters = expand.shape[1] // RANK
    picked = rows * RANK
    group_row = iota((rows, HD), 0)
    group_lane = iota((rows, HD), 1)
    chunks = expand.shape[2] // HD
    stack = recv_f.shape[1] // rows
    tiles = recv_f.shape[0]
    early = chunks // stack
    keep = lax.div(group_lane, RANK) == group_row
    wanted = jnp.zeros((2 * picked, HD), jnp.int32)
    pick_row = iota((2 * picked, HD), 0)
    for half in range(2):
        of_grp = 1 - grp if half == 0 else grp
        for i in range(rows):
            wanted = jnp.where(
                lax.div(pick_row, RANK) == half * rows + i,
                ids[of_grp * micro_rows + row * rows + i],
                wanted,
            )
    wanted = (wanted - grp * half_adapters) * RANK + lax.rem(pick_row, RANK)
    pick_lane = iota((2 * picked, HD), 1)
    pick = jnp.concatenate(
        [
            jnp.where(pick_lane + c * HD == wanted, 1.0, 0.0)
            for c in range(half_adapters * RANK // HD)
        ],
        axis=1,
    ).astype(BF16)
    for copy in expand_copies:
        copy.wait()
    for which in range(2):
        chosen_rows[which] = jnp.dot(
            pick, expand[which], preferred_element_type=F32
        ).astype(BF16)

    resid_copy.wait()
    gain_copy.wait()
    for copy in down_copies:
        copy.wait()
    wait_bytes(recv_d.at[0 : n_tp - 1], recv_sem.at[3])
    hidden = resid[...].astype(F32)
    projected = recv_d[0].astype(F32)
    for s in range(1, n_tp):
        projected += recv_d[s].astype(F32)
    hidden = hidden + projected
    stream_out[...] = hidden.astype(BF16)
    squares = jnp.sum(hidden * hidden, axis=1, keepdims=True)
    scaled = (hidden * gain[...].astype(F32).reshape(1, HD)).astype(BF16)

    def selected(table):
        product = jnp.dot(scaled, table, preferred_element_type=F32)
        per_chunk = HD // RANK
        chosen = jnp.zeros((micro_rows, HD), F32)
        for c in range(product.shape[1] // HD):
            chosen += jnp.where(
                lane_adapter + c * per_chunk == micro_ids, product[:, c * HD : (c + 1) * HD], 0.0
            )
        shift = HD // 2
        while shift >= RANK:
            chosen += pltpu.roll(chosen, shift, 1)
            shift //= 2
        return chosen

    lane = iota((micro_rows, HD), 1)
    own_row = lax.rem(iota((micro_rows, HD), 0), rows)
    ranks = jnp.where(
        lax.rem(lax.div(lane, RANK), 2) == 0, selected(down[0]), selected(down[1])
    )
    ranks = jnp.where(lax.div(lane, 2 * RANK) == own_row, ranks, 0.0)
    squares = jnp.where(lane == own_row, squares, 0.0)

    for r in range(n_row):
        of_group = slice(r * rows, (r + 1) * rows)
        send_e[r, 0:1] = jnp.sum(ranks[of_group], axis=0, keepdims=True)
        send_e[r, 1:2] = jnp.sum(squares[of_group], axis=0, keepdims=True)
    n_first = n_row * n_x
    for dr, dx in sorted(
        [(dr, dx) for dr in range(n_row) for dx in range(n_x) if dr or dx],
        key=lambda at: -min(at[0], n_row - at[0]) - min(at[1], n_x - at[1]),
    ):
        there = lax.rem(row + dr, n_row)
        remote(
            send_e.at[there],
            recv_e.at[dr * n_x + dx - 1],
            4,
            {"row": there, "tp": same_plane(dx)},
        ).start()
    recv_e[n_first - 1] = send_e[row]
    wait_bytes(recv_e.at[0 : n_first - 1], recv_sem.at[4])
    summed = recv_e[0]
    for s in range(1, n_first):
        summed += recv_e[s]

    recv_g[n_near - 1] = summed
    mine = recv_g.at[n_near - 1]

    @pl.when(grp == 0)
    def _():
        pl.semaphore_wait(answer, n_near)

    for i in range(n_near):
        remote(mine, recv_g.at[n_near + i], 6, {"grp": 1 - grp, "tp": same_column(i)}).start()
    for i in range(1, n_near):
        remote(mine, recv_g.at[i - 1], 5, {"tp": same_column(i)}).start()

    def expanded(half, first_slot):
        sums = recv_g[first_slot]
        for s in range(1, n_near):
            sums += recv_g[first_slot + s]
        norms = jnp.sum(
            jnp.where(group_lane == group_row, jnp.broadcast_to(sums[1:2], (rows, HD)), 0.0),
            axis=1,
            keepdims=True,
        )
        inverse = lax.rsqrt(norms / (n_row * n_tp * HD) + EPSILON)
        ranks = jnp.broadcast_to(sums[0:1], (rows, HD)) * inverse
        for which in range(2):
            spread_rank = jnp.where(
                lax.div(group_lane, RANK) == 2 * group_row + which, ranks, 0.0
            )
            shift = RANK
            while shift < HD:
                spread_rank += pltpu.roll(spread_rank, shift, 1)
                shift *= 2
            coefficient = jnp.where(keep, spread_rank, 0.0)[:, :picked]
            yield jnp.dot(
                coefficient.astype(BF16),
                chosen_rows[which, half * picked : (half + 1) * picked],
                preferred_element_type=F32,
            )

    wait_bytes(recv_g.at[n_near : 2 * n_near], recv_sem.at[6])
    pieces = []
    for which, delta in enumerate(expanded(0, n_near)):
        pieces += [delta[:, c * HD : (c + 1) * HD] for c in range(chunks)]
        if which:
            pieces += [jnp.zeros((rows, HD), F32)] * (-len(pieces) % stack)
        span = (early, tiles) if which else (0, early)
        for i in range(*span):
            send_f[i] = jnp.concatenate(pieces[i * stack : (i + 1) * stack], axis=0).astype(BF16)
        remote(
            send_f.at[span[0] : span[1]], recv_f.at[span[0] : span[1]], 7 + which, {"grp": 1 - grp}
        ).start()

    wait_bytes(recv_g.at[0 : n_near - 1], recv_sem.at[5])
    own = [delta.astype(BF16).astype(F32) for delta in expanded(1, 0)]
    outs = (gate_out, up_out)
    for which in range(2):
        for c in range(chunks):
            at = which * chunks + c
            if at == 0:
                wait_bytes(recv_f.at[0:early], recv_sem.at[7])
            if at == early * stack:
                wait_bytes(recv_f.at[early:tiles], recv_sem.at[8])
            other = recv_f[at // stack].astype(F32)[at % stack * rows : (at % stack + 1) * rows]
            columns = slice(c * HD, (c + 1) * HD)
            outs[which][:, columns] = (own[which][:, columns] + other).astype(BF16)

    wait_bytes(recv_b.at[0 : n_tp - 1], send_sem.at[0])
    wait_bytes(recv_st.at[0 : n_tp - 1], send_sem.at[1])
    wait_bytes(recv_c.at[0 : n_row - 1], send_sem.at[2])
    wait_bytes(recv_d.at[0 : n_tp - 1], send_sem.at[3])
    wait_bytes(recv_e.at[0 : n_first - 1], send_sem.at[4])
    wait_bytes(recv_g.at[0 : n_near - 1], send_sem.at[5])
    wait_bytes(recv_g.at[n_near : 2 * n_near], send_sem.at[6])
    wait_bytes(send_f.at[0:early], send_sem.at[7])
    wait_bytes(send_f.at[early:tiles], send_sem.at[8])


def hand_over(stream, gate, up, stream_out, gate_out, up_out, sem):
    copies = [
        pltpu.make_async_copy(source, target, sem.at[i])
        for i, (source, target) in enumerate(((stream, stream_out), (gate, gate_out), (up, up_out)))
    ]
    for copy in copies:
        copy.start()
    for copy in copies:
        copy.wait()


def layer(
    sizes,
    query,
    cached_key_rows,
    cached_value_rows,
    row_cache_length,
    attention_output_weight,
    resid,
    feed_norm_scale,
    gate_down_weight,
    up_down_weight,
    gate_expansion_weight,
    up_expansion_weight,
    row_adapter_index,
):
    n_grp, n_row, n_tp = sizes
    rows = query.shape[0]
    heads = query.shape[1] // HD
    tile = rows * (heads // n_tp)
    columns = gate_expansion_weight.shape[1]
    n_core = min(2, n_tp // 4)
    n_x = n_tp // 4 // n_core
    stack = 16 // rows
    packed = -(-2 * (columns // HD) // stack)
    hbm = pl.BlockSpec(memory_space=pl.ANY)
    vmem = pl.BlockSpec(memory_space=pltpu.VMEM)
    parts = pl.pallas_call(
        functools.partial(kernel, sizes),
        out_shape=(
            pltpu.VMEM(resid.shape, BF16),
            pltpu.VMEM((rows, columns), BF16),
            pltpu.VMEM((rows, columns), BF16),
        ),
        in_specs=[hbm] * 12,
        out_specs=(vmem,) * 3,
        scratch_shapes=[
            pltpu.SMEM(row_cache_length.shape, jnp.int32),
            pltpu.SMEM(row_adapter_index.shape, jnp.int32),
            pltpu.VMEM(query.shape, BF16),
            pltpu.VMEM(cached_key_rows.shape, BF16),
            pltpu.VMEM(cached_value_rows.shape, BF16),
            pltpu.VMEM(attention_output_weight.shape, BF16),
            pltpu.VMEM(resid.shape, BF16),
            pltpu.VMEM(feed_norm_scale.shape, BF16),
            pltpu.VMEM((2,) + gate_down_weight.shape, BF16),
            pltpu.VMEM((2,) + gate_expansion_weight.shape, BF16),
            pltpu.VMEM((rows, heads, cached_key_rows.shape[1]), BF16),
            pltpu.VMEM((rows, heads, HD), F32),
            pltpu.VMEM((n_tp, tile, HD), F32),
            pltpu.VMEM((heads, HD), F32),
            pltpu.VMEM((n_tp * tile, HD), F32),
            pltpu.VMEM((n_tp, tile, HD), BF16),
            pltpu.VMEM((n_tp, 1, HD), F32),
            pltpu.VMEM((n_tp, tile, HD), BF16),
            pltpu.VMEM((n_tp, 1, HD), F32),
            pltpu.VMEM((n_row, tile, HD), BF16),
            pltpu.VMEM((n_tp, n_row * rows, HD), BF16),
            pltpu.VMEM((n_tp, n_row * rows, HD), BF16),
            pltpu.VMEM((n_row, 2, HD), F32),
            pltpu.VMEM((n_row * n_x, 2, HD), F32),
            pltpu.VMEM((8 * n_core, 2, HD), F32),
            pltpu.VMEM((packed, 16, HD), BF16),
            pltpu.VMEM((packed, 16, HD), BF16),
            pltpu.VMEM((2, 2 * rows * RANK, columns), BF16),
            pltpu.SemaphoreType.DMA((10,)),
            pltpu.SemaphoreType.DMA((2, rows)),
            pltpu.SemaphoreType.DMA((9,)),
            pltpu.SemaphoreType.DMA((9,)),
            pltpu.SemaphoreType.REGULAR,
        ],
        compiler_params=pltpu.CompilerParams(
            collective_id=0, has_side_effects=True, vmem_limit_bytes=56 * 1024 * 1024
        ),
    )(
        row_cache_length,
        row_adapter_index,
        query,
        cached_key_rows,
        cached_value_rows,
        attention_output_weight,
        resid,
        feed_norm_scale,
        gate_down_weight,
        up_down_weight,
        gate_expansion_weight,
        up_expansion_weight,
    )
    return pl.pallas_call(
        hand_over,
        out_shape=tuple(jax.ShapeDtypeStruct(part.shape, part.dtype) for part in parts),
        in_specs=[hbm] * 3,
        out_specs=(pl.BlockSpec(memory_space=pltpu.HBM),) * 3,
        scratch_shapes=[pltpu.SemaphoreType.DMA((3,))],
            compiler_params=pltpu.CompilerParams(vmem_limit_bytes=1024 * 1024),
    )(*[pltpu.with_memory_space_constraint(p, pltpu.VMEM) for p in parts])


def solution(mesh):
    sizes = tuple(mesh.shape[axis] for axis in ("grp", "row", "tp"))
    return jax.shard_map(
        functools.partial(layer, sizes),
        mesh=mesh,
        in_specs=(
            P(("grp", "row"), None),
            P(("grp", "row"), "tp", None),
            P(("grp", "row"), "tp", None),
            P(("grp", "row")),
            P("tp", "row"),
            P("grp", ("row", "tp")),
            P(("row", "tp")),
            P(("row", "tp"), None),
            P(("row", "tp"), None),
            P("grp", "tp"),
            P("grp", "tp"),
            P(),
        ),
        out_specs=(P("grp", ("row", "tp")), P(("grp", "row"), "tp"), P(("grp", "row"), "tp")),
        check_vma=False,
    )
```

```python
import functools

import jax
import jax.numpy as jnp
from jax import lax
from jax.experimental import pallas as pl
from jax.experimental.pallas import tpu as pltpu
from jax.sharding import PartitionSpec as P

HD = 128
RANK = 16
EPSILON = 1e-05
MESH = pl.DeviceIdType.MESH
F32 = jnp.float32
BF16 = jnp.bfloat16


def iota(shape, axis):
    return lax.broadcasted_iota(jnp.int32, shape, axis)


def kernel(
    sizes,
    lengths_hbm,
    ids_hbm,
    query_hbm,
    key_hbm,
    value_hbm,
    wo_hbm,
    resid_hbm,
    gain_hbm,
    gate_down_hbm,
    up_down_hbm,
    gate_exp_hbm,
    up_exp_hbm,
    stream_out,
    gate_out,
    up_out,
    lengths,
    ids,
    query,
    keys,
    values,
    wo,
    resid,
    gain,
    down,
    expand,
    weights_s,
    acc_s,
    share_s,
    stat_s,
    msg_s,
    send_b,
    send_st,
    recv_b,
    recv_st,
    recv_c,
    send_d,
    recv_d,
    send_e,
    recv_e,
    recv_g,
    send_x,
    recv_x,
    send_f,
    recv_f,
    chosen_rows,
    load_sem,
    kv_sem,
    send_sem,
    recv_sem,
    answer,
):
    n_grp, n_row, n_tp = sizes
    rows, positions, kv_width = keys.shape
    kv_heads = kv_width // HD
    heads = query.shape[1] // HD
    group = heads // kv_heads
    per = heads // n_tp
    tile = rows * per
    micro_rows = n_row * rows
    grp = lax.axis_index("grp")
    row = lax.axis_index("row")
    me = lax.axis_index("tp")

    def load(source, target, index):
        copy = pltpu.make_async_copy(source, target, load_sem.at[index])
        copy.start()
        return copy

    def wait_bytes(ref, sem):
        pltpu.make_async_copy(ref, ref, sem).wait()

    quarter = n_tp // 4
    plane = lax.div(me, quarter)
    place = lax.rem(me, quarter)
    n_core = min(2, quarter)
    n_x = quarter // n_core
    place_x = lax.div(place, n_core)
    core = lax.rem(place, n_core)
    n_near = 4 * n_core

    def other_plane(turn):
        high = lax.rem(lax.div(plane, 2) + turn // 2, 2)
        return 2 * high + lax.rem(plane + turn % 2, 2)

    def ahead(there):
        return lax.rem(there - me + n_tp, n_tp)

    query_copy = load(query_hbm, query, 0)
    key_copies = [
        pltpu.make_async_copy(key_hbm.at[b], keys.at[b], kv_sem.at[0, b]) for b in range(rows)
    ]
    value_copies = [
        pltpu.make_async_copy(value_hbm.at[b], values.at[b], kv_sem.at[1, b]) for b in range(rows)
    ]
    in_order = key_copies + value_copies
    flying = rows + rows // 2
    for copy in in_order[:flying]:
        copy.start()

    lengths_copy = load(lengths_hbm, lengths, 8)
    ids_copy = load(ids_hbm, ids, 9)

    def arrived(first, count):
        for i in range(first, first + count):
            in_order[i].wait()
            if i + flying < 2 * rows:
                in_order[i + flying].start()

    barrier = pltpu.get_barrier_semaphore()

    def same_plane(dx):
        return plane * quarter + lax.rem(place_x + dx, n_x) * n_core + core

    def same_column(i):
        there = lax.rem(plane + i // n_core, 4) * quarter + place_x * n_core
        return there + lax.rem(core + i % n_core, n_core)

    def greet(k, carry):
        there = lax.rem(me + k, n_tp)
        pl.semaphore_signal(barrier, inc=1, device_id={"tp": there}, device_id_type=MESH)
        return carry

    @pl.when(grp == 0)
    def _():
        pl.semaphore_signal(barrier, inc=1, device_id={"grp": 1 - grp}, device_id_type=MESH)

    lax.fori_loop(1, n_tp, greet, 0)
    for k in range(1, n_row):
        pl.semaphore_signal(
            barrier, inc=1, device_id={"row": lax.rem(row + k, n_row)}, device_id_type=MESH
        )

    query_copy.wait()
    head_rows = query[...].astype(F32).reshape(rows, heads, HD).astype(BF16)
    position = me * positions + iota((heads, positions), 1)
    stat_lane = iota((heads, HD), 1) - rows * lax.rem(iota((heads, HD), 0), per)
    stats = jnp.zeros((heads, HD), F32)
    lengths_copy.wait()
    arrived(0, rows)
    for b in range(rows):
        scores = jnp.concatenate(
            [
                lax.dot_general(
                    head_rows[b, k * group : (k + 1) * group],
                    keys[b, :, k * HD : (k + 1) * HD],
                    (((1,), (1,)), ((), ())),
                    preferred_element_type=F32,
                )
                for k in range(kv_heads)
            ],
            axis=0,
        ) * (HD ** (-0.5))
        visible = position < lengths[b]
        masked = jnp.where(visible, scores, -1e30)
        highest = jnp.max(masked, axis=1, keepdims=True)
        weights = jnp.where(visible, jnp.exp(masked - highest), 0.0)
        total = jnp.sum(weights, axis=1, keepdims=True)
        weights_s[b] = weights.astype(BF16)
        stats = jnp.where(stat_lane == b, highest, stats)
        stats = jnp.where(stat_lane == tile + b, total, stats)
    stat_s[...] = stats
    stat_rows = stat_s[pl.ds(0, n_tp, stride=per), :]
    for j in range(1, per):
        stat_rows += stat_s[pl.ds(j, n_tp, stride=per), :]
    send_st[...] = stat_rows.reshape(n_tp, 1, HD)

    within = n_tp - 1 + n_row - 1

    @pl.when(grp == 0)
    def _():
        pl.semaphore_wait(barrier, within)

    @pl.when(grp == 1)
    def _():
        pl.semaphore_wait(barrier, within + 1)

    def answer_peer():
        pl.semaphore_signal(answer, inc=1, device_id={"grp": 1 - grp}, device_id_type=MESH)

    def remote(source, target, index, device):
        return pltpu.make_async_remote_copy(
            src_ref=source,
            dst_ref=target,
            send_sem=send_sem.at[index],
            recv_sem=recv_sem.at[index],
            device_id=device,
            device_id_type=MESH,
        )

    def send_stats(k, carry):
        there = lax.rem(me + k, n_tp)
        remote(send_st.at[there], recv_st.at[k - 1], 1, {"tp": there}).start()
        return carry

    lax.fori_loop(1, n_tp, send_stats, 0)
    recv_st[n_tp - 1] = send_st[me]
    wo_copy = load(wo_hbm, wo, 1)
    resid_copy = load(resid_hbm, resid, 2)
    gain_copy = load(gain_hbm, gain, 3)
    down_copies = (load(gate_down_hbm, down.at[0], 4), load(up_down_hbm, down.at[1], 5))
    expand_copies = (load(gate_exp_hbm, expand.at[0], 6), load(up_exp_hbm, expand.at[1], 7))

    for b in range(rows):
        if b % 2 == 0:
            arrived(rows + b, 2)
        weights = weights_s[b]
        for k in range(kv_heads):
            acc_s[b, k * group : (k + 1) * group, :] = jnp.dot(
                weights[k * group : (k + 1) * group],
                values[b, :, k * HD : (k + 1) * HD],
                preferred_element_type=F32,
            )
        for j in range(per):
            msg_s[pl.ds(j * rows + b, n_tp, stride=tile), :] = acc_s[
                b, pl.ds(j, n_tp, stride=per), :
            ]
    send_b[...] = msg_s[...].reshape(n_tp, tile, HD).astype(BF16)

    for turn in (3, 2, 1, 0):

        def send_partial(i, carry, turn=turn):
            there = other_plane(turn) * quarter + lax.rem(place + i, quarter)
            remote(send_b.at[there], recv_b.at[ahead(there) - 1], 0, {"tp": there}).start()
            return carry

        lax.fori_loop(0 if turn else 1, quarter, send_partial, 0)
    recv_b[n_tp - 1] = send_b[me]

    wait_bytes(recv_st.at[0 : n_tp - 1], recv_sem.at[1])
    part_stats = recv_st[...].reshape(n_tp, HD)
    overall = jnp.max(part_stats, axis=0, keepdims=True)
    factor = jnp.exp(part_stats - overall)
    part_totals = pltpu.roll(part_stats, HD - tile, 1)
    normal = jnp.sum(factor * part_totals, axis=0, keepdims=True)
    share = jnp.where(iota((n_tp, HD), 1) < tile, factor / normal, 0.0)
    share = share.T[:tile]
    for s in range(n_tp):
        share_s[s] = jnp.broadcast_to(share[:, s : s + 1], (tile, HD))
    wait_bytes(recv_b.at[0 : n_tp - 1], recv_sem.at[0])
    attended = share_s[0] * recv_b[0].astype(F32)
    for s in range(1, n_tp):
        attended += share_s[s] * recv_b[s].astype(F32)

    recv_c[row] = attended.astype(BF16)
    for k in range(1, n_row):
        remote(recv_c.at[row], recv_c.at[row], 2, {"row": lax.rem(row + k, n_row)}).start()
    wait_bytes(recv_c.at[0 : n_row - 1], recv_sem.at[2])

    @pl.when(grp == 1)
    def _():
        answer_peer()

    gathered = recv_c[...].astype(F32)
    left = jnp.concatenate(
        [
            jnp.concatenate(
                [gathered[r, j * rows : (j + 1) * rows] for r in range(n_row)], axis=0
            )
            for j in range(per)
        ],
        axis=1,
    ).astype(BF16)

    wo_copy.wait()
    for turn in (3, 2, 1, 0):
        first = other_plane(turn) * quarter
        columns = pl.ds(pl.multiple_of(first * HD, quarter * HD), quarter * HD)
        product = jnp.dot(left, wo[:, columns], preferred_element_type=F32).astype(BF16)
        for i in range(quarter):
            send_d[first + i] = product[:, i * HD : (i + 1) * HD]

        def send_sums(i, carry, first=first):
            there = first + lax.rem(place + i, quarter)
            remote(send_d.at[there], recv_d.at[ahead(there) - 1], 3, {"tp": there}).start()
            return carry

        lax.fori_loop(0 if turn else 1, quarter, send_sums, 0)

    recv_d[n_tp - 1] = send_d[me]

    def id_column(base, count, shape, start, column):
        for i in range(count):
            column = jnp.where(iota(shape, 0) == start + i, ids[base + i], column)
        return column

    ids_copy.wait()
    micro_ids = id_column(
        grp * micro_rows, micro_rows, (micro_rows, HD), 0, jnp.zeros((micro_rows, HD), jnp.int32)
    )
    lane_adapter = lax.div(iota((micro_rows, HD), 1), RANK)
    half_adapters = expand.shape[1] // RANK
    picked = rows * RANK
    group_row = iota((rows, HD), 0)
    group_lane = iota((rows, HD), 1)
    chunks = expand.shape[2] // HD
    stack = recv_f.shape[1] // rows
    tiles = recv_f.shape[0]
    early = chunks // stack
    keep = lax.div(group_lane, RANK) == group_row
    wanted = jnp.zeros((2 * picked, HD), jnp.int32)
    pick_row = iota((2 * picked, HD), 0)
    for half in range(2):
        of_grp = 1 - grp if half == 0 else grp
        for i in range(rows):
            wanted = jnp.where(
                lax.div(pick_row, RANK) == half * rows + i,
                ids[of_grp * micro_rows + row * rows + i],
                wanted,
            )
    wanted = (wanted - grp * half_adapters) * RANK + lax.rem(pick_row, RANK)
    pick_lane = iota((2 * picked, HD), 1)
    pick = jnp.concatenate(
        [
            jnp.where(pick_lane + c * HD == wanted, 1.0, 0.0)
            for c in range(half_adapters * RANK // HD)
        ],
        axis=1,
    ).astype(BF16)
    for copy in expand_copies:
        copy.wait()
    for which in range(2):
        chosen_rows[which] = jnp.dot(
            pick, expand[which], preferred_element_type=F32
        ).astype(BF16)

    @pl.when(grp == 0)
    def _():
        pl.semaphore_wait(answer, 1)
        answer_peer()

    resid_copy.wait()
    gain_copy.wait()
    for copy in down_copies:
        copy.wait()
    wait_bytes(recv_d.at[0 : n_tp - 1], recv_sem.at[3])
    hidden = resid[...].astype(F32)
    projected = recv_d[0].astype(F32)
    for s in range(1, n_tp):
        projected += recv_d[s].astype(F32)
    hidden = hidden + projected
    stream_out[...] = hidden.astype(BF16)
    squares = jnp.sum(hidden * hidden, axis=1, keepdims=True)
    scaled = (hidden * gain[...].astype(F32).reshape(1, HD)).astype(BF16)

    def selected(table):
        product = jnp.dot(scaled, table, preferred_element_type=F32)
        per_chunk = HD // RANK
        chosen = jnp.zeros((micro_rows, HD), F32)
        for c in range(product.shape[1] // HD):
            chosen += jnp.where(
                lane_adapter + c * per_chunk == micro_ids, product[:, c * HD : (c + 1) * HD], 0.0
            )
        shift = HD // 2
        while shift >= RANK:
            chosen += pltpu.roll(chosen, shift, 1)
            shift //= 2
        return chosen

    lane = iota((micro_rows, HD), 1)
    own_row = lax.rem(iota((micro_rows, HD), 0), rows)
    ranks = jnp.where(
        lax.rem(lax.div(lane, RANK), 2) == 0, selected(down[0]), selected(down[1])
    )
    ranks = jnp.where(lax.div(lane, 2 * RANK) == own_row, ranks, 0.0)
    squares = jnp.where(lane == own_row, squares, 0.0)

    for r in range(n_row):
        of_group = slice(r * rows, (r + 1) * rows)
        send_e[r, 0:1] = jnp.sum(ranks[of_group], axis=0, keepdims=True)
        send_e[r, 1:2] = jnp.sum(squares[of_group], axis=0, keepdims=True)
        send_x[r] = send_e[r, 0:1]

    @pl.when(grp == 1)
    def _():
        pl.semaphore_wait(answer, 1)

    for dr in (2, 1, 3, 0):
        to_row = lax.rem(row + dr, n_row)
        for turn in range(4):

            def send_ranks(i, carry, dr=dr, to_row=to_row, turn=turn):
                there = other_plane(turn) * quarter + lax.rem(place + quarter // 2 + i, quarter)
                remote(
                    send_x.at[to_row],
                    recv_x.at[dr * n_tp + ahead(there)],
                    6,
                    {"grp": 1 - grp, "row": to_row, "tp": there},
                ).start()
                return carry

            lax.fori_loop(0, quarter, send_ranks, 0)

    n_first = n_row * n_x
    for dr, dx in sorted(
        [(dr, dx) for dr in range(n_row) for dx in range(n_x) if dr or dx],
        key=lambda at: -min(at[0], n_row - at[0]) - min(at[1], n_x - at[1]),
    ):
        there = lax.rem(row + dr, n_row)
        remote(
            send_e.at[there],
            recv_e.at[dr * n_x + dx - 1],
            4,
            {"row": there, "tp": same_plane(dx)},
        ).start()
    recv_e[n_first - 1] = send_e[row]
    wait_bytes(recv_e.at[0 : n_first - 1], recv_sem.at[4])
    summed = recv_e[0]
    for s in range(1, n_first):
        summed += recv_e[s]

    recv_g[n_near - 1] = summed
    for i in range(1, n_near):
        remote(recv_g.at[n_near - 1], recv_g.at[i - 1], 5, {"tp": same_column(i)}).start()

    def expanded(half, ranks):
        for which in range(2):
            spread_rank = jnp.where(
                lax.div(group_lane, RANK) == 2 * group_row + which, ranks, 0.0
            )
            shift = RANK
            while shift < HD:
                spread_rank += pltpu.roll(spread_rank, shift, 1)
                shift *= 2
            coefficient = jnp.where(keep, spread_rank, 0.0)[:, :picked]
            yield jnp.dot(
                coefficient.astype(BF16),
                chosen_rows[which, half * picked : (half + 1) * picked],
                preferred_element_type=F32,
            )

    def added(ref, count):
        chains = [ref[s] for s in range(8)]
        for s in range(8, count):
            chains[s % 8] += ref[s]
        while len(chains) > 1:
            chains = [low + high for low, high in zip(chains[::2], chains[1::2])]
        return chains[0]

    wait_bytes(recv_x, recv_sem.at[6])
    other_ranks = jnp.broadcast_to(added(recv_x, n_row * n_tp), (rows, HD))
    pieces = []
    for which, delta in enumerate(expanded(0, other_ranks)):
        pieces += [delta[:, c * HD : (c + 1) * HD] for c in range(chunks)]
        if which:
            pieces += [jnp.zeros((rows, HD), F32)] * (-len(pieces) % stack)
        span = (early, tiles) if which else (0, early)
        for i in range(*span):
            send_f[i] = jnp.concatenate(pieces[i * stack : (i + 1) * stack], axis=0).astype(BF16)
        remote(
            send_f.at[span[0] : span[1]], recv_f.at[span[0] : span[1]], 7 + which, {"grp": 1 - grp}
        ).start()

    wait_bytes(recv_g.at[0 : n_near - 1], recv_sem.at[5])
    sums = recv_g[0]
    for s in range(1, n_near):
        sums += recv_g[s]
    norms = jnp.sum(
        jnp.where(group_lane == group_row, jnp.broadcast_to(sums[1:2], (rows, HD)), 0.0),
        axis=1,
        keepdims=True,
    )
    inverse = lax.rsqrt(norms / (n_row * n_tp * HD) + EPSILON)
    own_ranks = jnp.broadcast_to(sums[0:1], (rows, HD)) * inverse
    own = [delta.astype(BF16).astype(F32) for delta in expanded(1, own_ranks)]
    outs = (gate_out, up_out)
    for which in range(2):
        for c in range(chunks):
            at = which * chunks + c
            if at == 0:
                wait_bytes(recv_f.at[0:early], recv_sem.at[7])
            if at == early * stack:
                wait_bytes(recv_f.at[early:tiles], recv_sem.at[8])
            other = recv_f[at // stack].astype(F32)[at % stack * rows : (at % stack + 1) * rows]
            columns = slice(c * HD, (c + 1) * HD)
            outs[which][:, columns] = (own[which][:, columns] + other * inverse).astype(BF16)

    wait_bytes(recv_b.at[0 : n_tp - 1], send_sem.at[0])
    wait_bytes(recv_st.at[0 : n_tp - 1], send_sem.at[1])
    wait_bytes(recv_c.at[0 : n_row - 1], send_sem.at[2])
    wait_bytes(recv_d.at[0 : n_tp - 1], send_sem.at[3])
    wait_bytes(recv_e.at[0 : n_first - 1], send_sem.at[4])
    wait_bytes(recv_g.at[0 : n_near - 1], send_sem.at[5])
    wait_bytes(recv_x, send_sem.at[6])
    wait_bytes(send_f.at[0:early], send_sem.at[7])
    wait_bytes(send_f.at[early:tiles], send_sem.at[8])


def hand_over(stream, gate, up, stream_out, gate_out, up_out, sem):
    copies = [
        pltpu.make_async_copy(source, target, sem.at[i])
        for i, (source, target) in enumerate(((stream, stream_out), (gate, gate_out), (up, up_out)))
    ]
    for copy in copies:
        copy.start()
    for copy in copies:
        copy.wait()


def layer(
    sizes,
    query,
    cached_key_rows,
    cached_value_rows,
    row_cache_length,
    attention_output_weight,
    resid,
    feed_norm_scale,
    gate_down_weight,
    up_down_weight,
    gate_expansion_weight,
    up_expansion_weight,
    row_adapter_index,
):
    n_grp, n_row, n_tp = sizes
    rows = query.shape[0]
    heads = query.shape[1] // HD
    tile = rows * (heads // n_tp)
    columns = gate_expansion_weight.shape[1]
    n_core = min(2, n_tp // 4)
    n_x = n_tp // 4 // n_core
    stack = 16 // rows
    packed = -(-2 * (columns // HD) // stack)
    hbm = pl.BlockSpec(memory_space=pl.ANY)
    vmem = pl.BlockSpec(memory_space=pltpu.VMEM)
    parts = pl.pallas_call(
        functools.partial(kernel, sizes),
        out_shape=(
            pltpu.VMEM(resid.shape, BF16),
            pltpu.VMEM((rows, columns), BF16),
            pltpu.VMEM((rows, columns), BF16),
        ),
        in_specs=[hbm] * 12,
        out_specs=(vmem,) * 3,
        scratch_shapes=[
            pltpu.SMEM(row_cache_length.shape, jnp.int32),
            pltpu.SMEM(row_adapter_index.shape, jnp.int32),
            pltpu.VMEM(query.shape, BF16),
            pltpu.VMEM(cached_key_rows.shape, BF16),
            pltpu.VMEM(cached_value_rows.shape, BF16),
            pltpu.VMEM(attention_output_weight.shape, BF16),
            pltpu.VMEM(resid.shape, BF16),
            pltpu.VMEM(feed_norm_scale.shape, BF16),
            pltpu.VMEM((2,) + gate_down_weight.shape, BF16),
            pltpu.VMEM((2,) + gate_expansion_weight.shape, BF16),
            pltpu.VMEM((rows, heads, cached_key_rows.shape[1]), BF16),
            pltpu.VMEM((rows, heads, HD), F32),
            pltpu.VMEM((n_tp, tile, HD), F32),
            pltpu.VMEM((heads, HD), F32),
            pltpu.VMEM((n_tp * tile, HD), F32),
            pltpu.VMEM((n_tp, tile, HD), BF16),
            pltpu.VMEM((n_tp, 1, HD), F32),
            pltpu.VMEM((n_tp, tile, HD), BF16),
            pltpu.VMEM((n_tp, 1, HD), F32),
            pltpu.VMEM((n_row, tile, HD), BF16),
            pltpu.VMEM((n_tp, n_row * rows, HD), BF16),
            pltpu.VMEM((n_tp, n_row * rows, HD), BF16),
            pltpu.VMEM((n_row, 2, HD), F32),
            pltpu.VMEM((n_row * n_x, 2, HD), F32),
            pltpu.VMEM((4 * n_core, 2, HD), F32),
            pltpu.VMEM((n_row, 1, HD), F32),
            pltpu.VMEM((n_row * n_tp, 1, HD), F32),
            pltpu.VMEM((packed, 16, HD), BF16),
            pltpu.VMEM((packed, 16, HD), BF16),
            pltpu.VMEM((2, 2 * rows * RANK, columns), BF16),
            pltpu.SemaphoreType.DMA((10,)),
            pltpu.SemaphoreType.DMA((2, rows)),
            pltpu.SemaphoreType.DMA((9,)),
            pltpu.SemaphoreType.DMA((9,)),
            pltpu.SemaphoreType.REGULAR,
        ],
        compiler_params=pltpu.CompilerParams(
            collective_id=0, has_side_effects=True, vmem_limit_bytes=56 * 1024 * 1024
        ),
    )(
        row_cache_length,
        row_adapter_index,
        query,
        cached_key_rows,
        cached_value_rows,
        attention_output_weight,
        resid,
        feed_norm_scale,
        gate_down_weight,
        up_down_weight,
        gate_expansion_weight,
        up_expansion_weight,
    )
    return pl.pallas_call(
        hand_over,
        out_shape=tuple(jax.ShapeDtypeStruct(part.shape, part.dtype) for part in parts),
        in_specs=[hbm] * 3,
        out_specs=(pl.BlockSpec(memory_space=pltpu.HBM),) * 3,
        scratch_shapes=[pltpu.SemaphoreType.DMA((3,))],
            compiler_params=pltpu.CompilerParams(vmem_limit_bytes=1024 * 1024),
    )(*[pltpu.with_memory_space_constraint(p, pltpu.VMEM) for p in parts])


def solution(mesh):
    sizes = tuple(mesh.shape[axis] for axis in ("grp", "row", "tp"))
    return jax.shard_map(
        functools.partial(layer, sizes),
        mesh=mesh,
        in_specs=(
            P(("grp", "row"), None),
            P(("grp", "row"), "tp", None),
            P(("grp", "row"), "tp", None),
            P(("grp", "row")),
            P("tp", "row"),
            P("grp", ("row", "tp")),
            P(("row", "tp")),
            P(("row", "tp"), None),
            P(("row", "tp"), None),
            P("grp", "tp"),
            P("grp", "tp"),
            P(),
        ),
        out_specs=(P("grp", ("row", "tp")), P(("grp", "row"), "tp"), P(("grp", "row"), "tp")),
        check_vma=False,
    )
```

```python
import functools

import jax
import jax.numpy as jnp
from jax import lax
from jax.experimental import pallas as pl
from jax.experimental.pallas import tpu as pltpu
from jax.sharding import PartitionSpec as P

HD = 128
RANK = 16
EPSILON = 1e-05
MESH = pl.DeviceIdType.MESH
F32 = jnp.float32
BF16 = jnp.bfloat16


def iota(shape, axis):
    return lax.broadcasted_iota(jnp.int32, shape, axis)


def kernel(
    sizes,
    lengths_hbm,
    ids_hbm,
    query_hbm,
    key_hbm,
    value_hbm,
    wo_hbm,
    resid_hbm,
    gain_hbm,
    gate_down_hbm,
    up_down_hbm,
    gate_exp_hbm,
    up_exp_hbm,
    stream_out,
    gate_out,
    up_out,
    lengths,
    ids,
    query,
    keys,
    values,
    wo,
    resid,
    gain,
    down,
    expand,
    weights_s,
    acc_s,
    share_s,
    stat_s,
    msg_s,
    send_b,
    send_st,
    recv_b,
    recv_st,
    recv_c,
    send_d,
    recv_d,
    send_e,
    recv_e,
    recv_g,
    send_x,
    recv_x,
    send_f,
    recv_f,
    chosen_rows,
    load_sem,
    kv_sem,
    send_sem,
    recv_sem,
    answer,
):
    n_grp, n_row, n_tp = sizes
    rows, positions, kv_width = keys.shape
    kv_heads = kv_width // HD
    heads = query.shape[1] // HD
    group = heads // kv_heads
    per = heads // n_tp
    tile = rows * per
    micro_rows = n_row * rows
    grp = lax.axis_index("grp")
    row = lax.axis_index("row")
    me = lax.axis_index("tp")

    def load(source, target, index):
        copy = pltpu.make_async_copy(source, target, load_sem.at[index])
        copy.start()
        return copy

    def wait_bytes(ref, sem):
        pltpu.make_async_copy(ref, ref, sem).wait()

    quarter = n_tp // 4
    plane = lax.div(me, quarter)
    place = lax.rem(me, quarter)
    n_core = min(2, quarter)
    n_x = quarter // n_core
    place_x = lax.div(place, n_core)
    core = lax.rem(place, n_core)
    n_near = 4 * n_core

    def other_plane(turn):
        high = lax.rem(lax.div(plane, 2) + turn // 2, 2)
        return 2 * high + lax.rem(plane + turn % 2, 2)

    def ahead(there):
        return lax.rem(there - me + n_tp, n_tp)

    def added(terms):
        chains = terms[:4]
        for at, term in enumerate(terms[4:]):
            chains[at % 4] += term
        while len(chains) > 1:
            chains = [low + high for low, high in zip(chains[::2], chains[1::2])]
        return chains[0]

    query_copy = load(query_hbm, query, 0)
    key_copies = [
        pltpu.make_async_copy(key_hbm.at[b], keys.at[b], kv_sem.at[0, b]) for b in range(rows)
    ]
    value_copies = [
        pltpu.make_async_copy(value_hbm.at[b], values.at[b], kv_sem.at[1, b]) for b in range(rows)
    ]
    in_order = key_copies + value_copies
    flying = rows + rows // 2
    for copy in in_order[:flying]:
        copy.start()

    lengths_copy = load(lengths_hbm, lengths, 8)
    ids_copy = load(ids_hbm, ids, 9)

    def arrived(first, count):
        for i in range(first, first + count):
            in_order[i].wait()
            if i + flying < 2 * rows:
                in_order[i + flying].start()

    barrier = pltpu.get_barrier_semaphore()

    def same_plane(dx):
        return plane * quarter + lax.rem(place_x + dx, n_x) * n_core + core

    def same_column(i):
        there = lax.rem(plane + i // n_core, 4) * quarter + place_x * n_core
        return there + lax.rem(core + i % n_core, n_core)

    def greet(k, carry):
        there = lax.rem(me + k, n_tp)
        pl.semaphore_signal(barrier, inc=1, device_id={"tp": there}, device_id_type=MESH)
        return carry

    @pl.when(grp == 0)
    def _():
        pl.semaphore_signal(barrier, inc=1, device_id={"grp": 1 - grp}, device_id_type=MESH)

    lax.fori_loop(1, n_tp, greet, 0)
    for k in range(1, n_row):
        pl.semaphore_signal(
            barrier, inc=1, device_id={"row": lax.rem(row + k, n_row)}, device_id_type=MESH
        )

    query_copy.wait()
    head_rows = query[...].astype(F32).reshape(rows, heads, HD).astype(BF16)
    position = me * positions + iota((heads, positions), 1)
    stat_lane = iota((heads, HD), 1) - rows * lax.rem(iota((heads, HD), 0), per)
    stats = jnp.zeros((heads, HD), F32)
    lengths_copy.wait()
    arrived(0, rows)
    for b in range(rows):
        scores = jnp.concatenate(
            [
                lax.dot_general(
                    head_rows[b, k * group : (k + 1) * group],
                    keys[b, :, k * HD : (k + 1) * HD],
                    (((1,), (1,)), ((), ())),
                    preferred_element_type=F32,
                )
                for k in range(kv_heads)
            ],
            axis=0,
        ) * (HD ** (-0.5))
        visible = position < lengths[b]
        masked = jnp.where(visible, scores, -1e30)
        highest = jnp.max(masked, axis=1, keepdims=True)
        weights = jnp.where(visible, jnp.exp(masked - highest), 0.0)
        total = jnp.sum(weights, axis=1, keepdims=True)
        weights_s[b] = weights.astype(BF16)
        stats = jnp.where(stat_lane == b, highest, stats)
        stats = jnp.where(stat_lane == tile + b, total, stats)
    stat_s[...] = stats
    stat_rows = stat_s[pl.ds(0, n_tp, stride=per), :]
    for j in range(1, per):
        stat_rows += stat_s[pl.ds(j, n_tp, stride=per), :]
    send_st[...] = stat_rows.reshape(n_tp, 1, HD)

    within = n_tp - 1 + n_row - 1

    @pl.when(grp == 0)
    def _():
        pl.semaphore_wait(barrier, within)

    def answer_peer(which):
        pl.semaphore_signal(
            answer.at[which], inc=1, device_id={"grp": 1 - grp}, device_id_type=MESH
        )

    @pl.when(grp == 1)
    def _():
        pl.semaphore_wait(barrier, within + 1)
        answer_peer(0)

    def remote(source, target, index, device):
        return pltpu.make_async_remote_copy(
            src_ref=source,
            dst_ref=target,
            send_sem=send_sem.at[index],
            recv_sem=recv_sem.at[index],
            device_id=device,
            device_id_type=MESH,
        )

    def send_stats(k, carry):
        there = lax.rem(me + k, n_tp)
        remote(send_st.at[there], recv_st.at[k - 1], 1, {"tp": there}).start()
        return carry

    lax.fori_loop(1, n_tp, send_stats, 0)
    recv_st[n_tp - 1] = send_st[me]
    for b in range(rows):
        if b % 2 == 0:
            arrived(rows + b, 2)
        weights = weights_s[b]
        for k in range(kv_heads):
            acc_s[b, k * group : (k + 1) * group, :] = jnp.dot(
                weights[k * group : (k + 1) * group],
                values[b, :, k * HD : (k + 1) * HD],
                preferred_element_type=F32,
            )
        for j in range(per):
            msg_s[pl.ds(j * rows + b, n_tp, stride=tile), :] = acc_s[
                b, pl.ds(j, n_tp, stride=per), :
            ]
    send_b[...] = msg_s[...].reshape(n_tp, tile, HD).astype(BF16)

    for turn in (3, 2, 1, 0):

        def send_partial(i, carry, turn=turn):
            there = other_plane(turn) * quarter + lax.rem(place + i, quarter)
            remote(send_b.at[there], recv_b.at[ahead(there) - 1], 0, {"tp": there}).start()
            return carry

        lax.fori_loop(0 if turn else 1, quarter, send_partial, 0)
    wo_copy = load(wo_hbm, wo, 1)
    resid_copy = load(resid_hbm, resid, 2)
    gain_copy = load(gain_hbm, gain, 3)
    down_copies = (load(gate_down_hbm, down.at[0], 4), load(up_down_hbm, down.at[1], 5))
    expand_copies = (load(gate_exp_hbm, expand.at[0], 6), load(up_exp_hbm, expand.at[1], 7))
    recv_b[n_tp - 1] = send_b[me]

    wait_bytes(recv_st.at[0 : n_tp - 1], recv_sem.at[1])
    part_stats = recv_st[...].reshape(n_tp, HD)
    overall = jnp.max(part_stats, axis=0, keepdims=True)
    factor = jnp.exp(part_stats - overall)
    part_totals = pltpu.roll(part_stats, HD - tile, 1)
    normal = jnp.sum(factor * part_totals, axis=0, keepdims=True)
    share = jnp.where(iota((n_tp, HD), 1) < tile, factor / normal, 0.0)
    share = share.T[:tile]
    for s in range(n_tp):
        share_s[s] = jnp.broadcast_to(share[:, s : s + 1], (tile, HD))
    wait_bytes(recv_b.at[0 : n_tp - 1], recv_sem.at[0])
    attended = added([share_s[s] * recv_b[s].astype(F32) for s in range(n_tp)])

    recv_c[row] = attended.astype(BF16)
    for k in range(1, n_row):
        remote(recv_c.at[row], recv_c.at[row], 2, {"row": lax.rem(row + k, n_row)}).start()
    wait_bytes(recv_c.at[0 : n_row - 1], recv_sem.at[2])

    @pl.when(grp == 0)
    def _():
        pl.semaphore_wait(answer.at[0], 1)

    answer_peer(1)

    gathered = recv_c[...].astype(F32)
    left = jnp.concatenate(
        [
            jnp.concatenate(
                [gathered[r, j * rows : (j + 1) * rows] for r in range(n_row)], axis=0
            )
            for j in range(per)
        ],
        axis=1,
    ).astype(BF16)

    wo_copy.wait()
    for turn in (3, 2, 1, 0):
        first = other_plane(turn) * quarter
        columns = pl.ds(pl.multiple_of(first * HD, quarter * HD), quarter * HD)
        product = jnp.dot(left, wo[:, columns], preferred_element_type=F32).astype(BF16)
        for i in range(quarter):
            send_d[first + i] = product[:, i * HD : (i + 1) * HD]

        def send_sums(i, carry, first=first):
            there = first + lax.rem(place + i, quarter)
            remote(send_d.at[there], recv_d.at[ahead(there) - 1], 3, {"tp": there}).start()
            return carry

        lax.fori_loop(0 if turn else 1, quarter, send_sums, 0)

    recv_d[n_tp - 1] = send_d[me]

    def id_column(base, count, shape, start, column):
        for i in range(count):
            column = jnp.where(iota(shape, 0) == start + i, ids[base + i], column)
        return column

    ids_copy.wait()
    micro_ids = id_column(
        grp * micro_rows, micro_rows, (micro_rows, HD), 0, jnp.zeros((micro_rows, HD), jnp.int32)
    )
    lane_adapter = lax.div(iota((micro_rows, HD), 1), RANK)
    half_adapters = expand.shape[1] // RANK
    picked = 2 * rows * RANK
    group_row = iota((rows, HD), 0)
    group_lane = iota((rows, HD), 1)
    chunks = expand.shape[2] // HD
    stack = recv_f.shape[1] // rows
    tiles = recv_f.shape[0]
    early = chunks // stack
    wanted = jnp.zeros((2 * picked, HD), jnp.int32)
    pick_row = iota((2 * picked, HD), 0)
    for half in range(2):
        of_grp = 1 - grp if half == 0 else grp
        for i in range(rows):
            wanted = jnp.where(
                lax.div(pick_row, 2 * RANK) == half * rows + i,
                ids[of_grp * micro_rows + row * rows + i],
                wanted,
            )
    wanted = (wanted - grp * half_adapters) * RANK + lax.rem(pick_row, RANK)
    pick_lane = iota((2 * picked, HD), 1)
    pick = jnp.concatenate(
        [
            jnp.where(pick_lane + c * HD == wanted, 1.0, 0.0)
            for c in range(half_adapters * RANK // HD)
        ],
        axis=1,
    ).astype(BF16)
    for copy in expand_copies:
        copy.wait()
    for which in range(2):
        chosen_rows[which] = jnp.dot(
            pick, expand[which], preferred_element_type=F32
        ).astype(BF16)

    resid_copy.wait()
    gain_copy.wait()
    for copy in down_copies:
        copy.wait()
    wait_bytes(recv_d.at[0 : n_tp - 1], recv_sem.at[3])
    hidden = resid[...].astype(F32)
    hidden = hidden + added([recv_d[s].astype(F32) for s in range(n_tp)])
    stream_out[...] = hidden.astype(BF16)
    squares = jnp.sum(hidden * hidden, axis=1, keepdims=True)
    scaled = (hidden * gain[...].astype(F32).reshape(1, HD)).astype(BF16)

    def selected(table):
        product = jnp.dot(scaled, table, preferred_element_type=F32)
        per_chunk = HD // RANK
        chosen = jnp.zeros((micro_rows, HD), F32)
        for c in range(product.shape[1] // HD):
            chosen += jnp.where(
                lane_adapter + c * per_chunk == micro_ids, product[:, c * HD : (c + 1) * HD], 0.0
            )
        shift = HD // 2
        while shift >= RANK:
            chosen += pltpu.roll(chosen, shift, 1)
            shift //= 2
        return chosen

    lane = iota((micro_rows, HD), 1)
    own_row = lax.rem(iota((micro_rows, HD), 0), rows)
    ranks = jnp.where(
        lax.rem(lax.div(lane, RANK), 2) == 0, selected(down[0]), selected(down[1])
    )
    ranks = jnp.where(lax.div(lane, 2 * RANK) == own_row, ranks, 0.0)
    squares = jnp.where(lane == own_row, squares, 0.0)

    for r in range(n_row):
        of_group = slice(r * rows, (r + 1) * rows)
        send_e[r, 0:1] = jnp.sum(ranks[of_group], axis=0, keepdims=True)
        send_e[r, 1:2] = jnp.sum(squares[of_group], axis=0, keepdims=True)
        send_x[r] = send_e[r, 0:1]

    n_first = n_row * n_x
    for dr, dx in sorted(
        [(dr, dx) for dr in range(n_row) for dx in range(n_x) if dr or dx],
        key=lambda at: -min(at[0], n_row - at[0]) - min(at[1], n_x - at[1]),
    ):
        there = lax.rem(row + dr, n_row)
        remote(
            send_e.at[there],
            recv_e.at[dr * n_x + dx - 1],
            4,
            {"row": there, "tp": same_plane(dx)},
        ).start()

    pl.semaphore_wait(answer.at[1], 1)

    for turn, dr in ((0, 2), (0, 1), (0, 3), (1, 2), (1, 1), (1, 3), (0, 0), (3, 2),
                     (2, 2), (3, 1), (3, 3), (2, 1), (2, 3), (1, 0), (3, 0), (2, 0)):
        to_row = lax.rem(row + dr, n_row)

        def send_ranks(i, carry, dr=dr, to_row=to_row, turn=turn):
            there = other_plane(turn) * quarter + lax.rem(place + quarter // 2 + i, quarter)
            remote(
                send_x.at[to_row],
                recv_x.at[dr * n_tp + ahead(there)],
                6,
                {"grp": 1 - grp, "row": to_row, "tp": there},
            ).start()
            return carry

        lax.fori_loop(0, quarter, send_ranks, 0)

    recv_e[n_first - 1] = send_e[row]
    wait_bytes(recv_e.at[0 : n_first - 1], recv_sem.at[4])
    summed = added([recv_e[s] for s in range(n_first)])

    recv_g[n_near - 1] = summed
    for i in range(1, n_near):
        remote(recv_g.at[n_near - 1], recv_g.at[i - 1], 5, {"tp": same_column(i)}).start()

    def expanded(half, ranks):
        for which in range(2):
            mine = lax.div(group_lane, RANK) == 2 * group_row + which
            yield jnp.dot(
                jnp.where(mine, ranks, 0.0).astype(BF16),
                chosen_rows[which, half * picked : (half + 1) * picked],
                preferred_element_type=F32,
            )

    wait_bytes(recv_x, recv_sem.at[6])
    other_ranks = jnp.broadcast_to(added([recv_x[s] for s in range(n_row * n_tp)]), (rows, HD))
    pieces = []
    for which, delta in enumerate(expanded(0, other_ranks)):
        pieces += [delta[:, c * HD : (c + 1) * HD] for c in range(chunks)]
        if which:
            pieces += [jnp.zeros((rows, HD), F32)] * (-len(pieces) % stack)
        span = (early, tiles) if which else (0, early)
        for i in range(*span):
            send_f[i] = jnp.concatenate(pieces[i * stack : (i + 1) * stack], axis=0).astype(BF16)
        remote(
            send_f.at[span[0] : span[1]], recv_f.at[span[0] : span[1]], 7 + which, {"grp": 1 - grp}
        ).start()

    wait_bytes(recv_g.at[0 : n_near - 1], recv_sem.at[5])
    sums = added([recv_g[s] for s in range(n_near)])
    norms = jnp.sum(
        jnp.where(group_lane == group_row, jnp.broadcast_to(sums[1:2], (rows, HD)), 0.0),
        axis=1,
        keepdims=True,
    )
    inverse = lax.rsqrt(norms / (n_row * n_tp * HD) + EPSILON)
    own_ranks = jnp.broadcast_to(sums[0:1], (rows, HD)) * inverse
    own = [delta.astype(BF16).astype(F32) for delta in expanded(1, own_ranks)]
    outs = (gate_out, up_out)
    for which in range(2):
        for c in range(chunks):
            at = which * chunks + c
            if at == 0:
                wait_bytes(recv_f.at[0:early], recv_sem.at[7])
            if at == early * stack:
                wait_bytes(recv_f.at[early:tiles], recv_sem.at[8])
            other = recv_f[at // stack].astype(F32)[at % stack * rows : (at % stack + 1) * rows]
            columns = slice(c * HD, (c + 1) * HD)
            outs[which][:, columns] = (own[which][:, columns] + other * inverse).astype(BF16)

    wait_bytes(recv_b.at[0 : n_tp - 1], send_sem.at[0])
    wait_bytes(recv_st.at[0 : n_tp - 1], send_sem.at[1])
    wait_bytes(recv_c.at[0 : n_row - 1], send_sem.at[2])
    wait_bytes(recv_d.at[0 : n_tp - 1], send_sem.at[3])
    wait_bytes(recv_e.at[0 : n_first - 1], send_sem.at[4])
    wait_bytes(recv_g.at[0 : n_near - 1], send_sem.at[5])
    wait_bytes(recv_x, send_sem.at[6])
    wait_bytes(send_f.at[0:early], send_sem.at[7])
    wait_bytes(send_f.at[early:tiles], send_sem.at[8])


def hand_over(stream, gate, up, stream_out, gate_out, up_out, sem):
    copies = [
        pltpu.make_async_copy(source, target, sem.at[i])
        for i, (source, target) in enumerate(((stream, stream_out), (gate, gate_out), (up, up_out)))
    ]
    for copy in copies:
        copy.start()
    for copy in copies:
        copy.wait()


def layer(
    sizes,
    query,
    cached_key_rows,
    cached_value_rows,
    row_cache_length,
    attention_output_weight,
    resid,
    feed_norm_scale,
    gate_down_weight,
    up_down_weight,
    gate_expansion_weight,
    up_expansion_weight,
    row_adapter_index,
):
    n_grp, n_row, n_tp = sizes
    rows = query.shape[0]
    heads = query.shape[1] // HD
    tile = rows * (heads // n_tp)
    columns = gate_expansion_weight.shape[1]
    n_core = min(2, n_tp // 4)
    n_x = n_tp // 4 // n_core
    stack = 16 // rows
    packed = -(-2 * (columns // HD) // stack)
    hbm = pl.BlockSpec(memory_space=pl.ANY)
    vmem = pl.BlockSpec(memory_space=pltpu.VMEM)
    parts = pl.pallas_call(
        functools.partial(kernel, sizes),
        out_shape=(
            pltpu.VMEM(resid.shape, BF16),
            pltpu.VMEM((rows, columns), BF16),
            pltpu.VMEM((rows, columns), BF16),
        ),
        in_specs=[hbm] * 12,
        out_specs=(vmem,) * 3,
        scratch_shapes=[
            pltpu.SMEM(row_cache_length.shape, jnp.int32),
            pltpu.SMEM(row_adapter_index.shape, jnp.int32),
            pltpu.VMEM(query.shape, BF16),
            pltpu.VMEM(cached_key_rows.shape, BF16),
            pltpu.VMEM(cached_value_rows.shape, BF16),
            pltpu.VMEM(attention_output_weight.shape, BF16),
            pltpu.VMEM(resid.shape, BF16),
            pltpu.VMEM(feed_norm_scale.shape, BF16),
            pltpu.VMEM((2,) + gate_down_weight.shape, BF16),
            pltpu.VMEM((2,) + gate_expansion_weight.shape, BF16),
            pltpu.VMEM((rows, heads, cached_key_rows.shape[1]), BF16),
            pltpu.VMEM((rows, heads, HD), F32),
            pltpu.VMEM((n_tp, tile, HD), F32),
            pltpu.VMEM((heads, HD), F32),
            pltpu.VMEM((n_tp * tile, HD), F32),
            pltpu.VMEM((n_tp, tile, HD), BF16),
            pltpu.VMEM((n_tp, 1, HD), F32),
            pltpu.VMEM((n_tp, tile, HD), BF16),
            pltpu.VMEM((n_tp, 1, HD), F32),
            pltpu.VMEM((n_row, tile, HD), BF16),
            pltpu.VMEM((n_tp, n_row * rows, HD), BF16),
            pltpu.VMEM((n_tp, n_row * rows, HD), BF16),
            pltpu.VMEM((n_row, 2, HD), F32),
            pltpu.VMEM((n_row * n_x, 2, HD), F32),
            pltpu.VMEM((4 * n_core, 2, HD), F32),
            pltpu.VMEM((n_row, 1, HD), F32),
            pltpu.VMEM((n_row * n_tp, 1, HD), F32),
            pltpu.VMEM((packed, 16, HD), BF16),
            pltpu.VMEM((packed, 16, HD), BF16),
            pltpu.VMEM((2, 4 * rows * RANK, columns), BF16),
            pltpu.SemaphoreType.DMA((10,)),
            pltpu.SemaphoreType.DMA((2, rows)),
            pltpu.SemaphoreType.DMA((9,)),
            pltpu.SemaphoreType.DMA((9,)),
            pltpu.SemaphoreType.REGULAR((2,)),
        ],
        compiler_params=pltpu.CompilerParams(
            collective_id=0, has_side_effects=True, vmem_limit_bytes=56 * 1024 * 1024
        ),
    )(
        row_cache_length,
        row_adapter_index,
        query,
        cached_key_rows,
        cached_value_rows,
        attention_output_weight,
        resid,
        feed_norm_scale,
        gate_down_weight,
        up_down_weight,
        gate_expansion_weight,
        up_expansion_weight,
    )
    return pl.pallas_call(
        hand_over,
        out_shape=tuple(jax.ShapeDtypeStruct(part.shape, part.dtype) for part in parts),
        in_specs=[hbm] * 3,
        out_specs=(pl.BlockSpec(memory_space=pltpu.HBM),) * 3,
        scratch_shapes=[pltpu.SemaphoreType.DMA((3,))],
            compiler_params=pltpu.CompilerParams(vmem_limit_bytes=1024 * 1024),
    )(*[pltpu.with_memory_space_constraint(p, pltpu.VMEM) for p in parts])


def solution(mesh):
    sizes = tuple(mesh.shape[axis] for axis in ("grp", "row", "tp"))
    return jax.shard_map(
        functools.partial(layer, sizes),
        mesh=mesh,
        in_specs=(
            P(("grp", "row"), None),
            P(("grp", "row"), "tp", None),
            P(("grp", "row"), "tp", None),
            P(("grp", "row")),
            P("tp", "row"),
            P("grp", ("row", "tp")),
            P(("row", "tp")),
            P(("row", "tp"), None),
            P(("row", "tp"), None),
            P("grp", "tp"),
            P("grp", "tp"),
            P(),
        ),
        out_specs=(P("grp", ("row", "tp")), P(("grp", "row"), "tp"), P(("grp", "row"), "tp")),
        check_vma=False,
    )
```
